32 devices in a mesh: groups: 2 (over y), clus: 4 (over z), pair: 2 (over x), rhs: 2 (over core).
Axes of the slice: x: 2, y: 2, z: 4, core: 2. Of those that a mesh axis runs over, the one named last changes fastest.
Arguments:
- rhs_field: float32 [16, 16384], P('rhs', ('groups', 'clus')), parts along dimension 1, may hold values from -6 to 6
- coefficients: float32 [4], replicated, may hold values from -1 to 1
- near_blocks: bfloat16 [256, 256, 256], P(('groups', 'clus', 'pair')), parts along dimension 0, may hold values from -0.125 to 0.125
- near_tgt: int32 [256], P(('groups', 'clus', 'pair')), parts along dimension 0, may hold values from 0 to 31, as said below
- near_src: int32 [256], P(('groups', 'clus', 'pair')), parts along dimension 0, may hold values from 0 to 31, as said below
- row_basis: bfloat16 [64, 16, 256], P(('groups', 'clus')), parts along dimension 0, may hold values from -0.25 to 0.25
- col_basis: bfloat16 [1024, 16, 256], P(('groups', 'clus', 'pair')), parts along dimension 0, may hold values from -0.375 to 0.375
- far_src: int32 [1024], P(('groups', 'clus', 'pair')), parts along dimension 0, may hold values from 0 to 31, as said below
- far_tgt: int32 [1024], P(('groups', 'clus', 'pair')), parts along dimension 0, may hold values from 0 to 31, as said below
Outputs:
- preconditioned: float32 [16, 16384], P('rhs', ('groups', 'clus')), parts along dimension 1
The draws below stay inside these ranges and needn't reach their ends.
There are 2 independent parts, one for each index of `groups`. The reference program is written for one: setup_inputs(seed, part) draws one part's arguments, and reference() takes and returns one part's arrays. A program takes and returns all parts, laid end to end along the dimension named above; an argument that names none is the same for every part. Nothing has to cross between parts.
Inputs may be any that keep to these rules, and one draw needn't show every extreme that they name: `near_tgt`: the rows are in aligned blocks of 16, one a device in the order of clus then pair; the block of clus index c names clusters c * 8 to (c + 1) * 8 - 1. `near_src`: in each aligned block of 16 rows (one a device, clus then pair, clus index c), exactly 2 rows name clusters of clus index c - 1 and exactly 2 name clusters of clus index c + 1 (both taken modulo the number of clus indices; cluster // 8 is a cluster's clus index), and all others name clusters of clus index c. `far_src`: the rows are in aligned blocks of 64, one a device in the order of clus then pair; the block of clus index c names clusters c * 8 to (c + 1) * 8 - 1. `far_tgt`: never equal to far_src of the same row.
All inputs are finite; a program needn't handle non-finite values.
Results may differ from the reference program's by a relative error of at most 0.0047.
Values may be sent and summed in bfloat16 or wider, within the bound.
A program may use at most 64 MiB of HBM per device.

```python
import jax
import jax.numpy as jnp
from jax import lax

LEAF = 256
R = 16
RHS = 16
DEG = 3
CL_DEV = 8
NB_DEV = 16
NF_DEV = 64
NCL = 32
PANELS = 8192
NNEAR = 128
NFAR = 512
CAP = 2
NEAR_PER = 4
FAR_PER = 16
N_CLUS = 4
N_PAIR = 2


def draw_near_tgt(key, part):
    owner_index = jnp.arange(NNEAR) // (NB_DEV * N_PAIR)
    chosen = jax.random.randint(jax.random.fold_in(key, 11), (NNEAR,), 0, CL_DEV)
    return (owner_index * CL_DEV + chosen).astype(jnp.int32)


def draw_near_src(key, part):
    device_total = N_CLUS * N_PAIR
    own_index = jnp.arange(device_total) // N_PAIR
    local_count = NB_DEV - 2 * CAP
    own_ids = jnp.broadcast_to(own_index[:, None], (device_total, local_count))
    down_ids = jnp.broadcast_to(((own_index + N_CLUS - 1) % N_CLUS)[:, None], (device_total, CAP))
    up_ids = jnp.broadcast_to(((own_index + 1) % N_CLUS)[:, None], (device_total, CAP))
    device_ids = jnp.concatenate([own_ids, down_ids, up_ids], axis=1)
    second_keys = jax.random.split(jax.random.fold_in(key, 29), device_total)
    arrange = jax.vmap(lambda sub_key: jax.random.permutation(sub_key, NB_DEV))(second_keys)
    device_ids = jnp.take_along_axis(device_ids, arrange, axis=1)
    chosen = jax.random.randint(jax.random.fold_in(key, 31), (device_total, NB_DEV), 0, CL_DEV)
    return (device_ids * CL_DEV + chosen).reshape(NNEAR).astype(jnp.int32)


def far_pairs(key):
    owner_index = jnp.arange(NFAR) // (NF_DEV * N_PAIR)
    chosen = jax.random.randint(jax.random.fold_in(key, 41), (NFAR,), 0, CL_DEV)
    anchor = owner_index * CL_DEV + chosen
    offset = jax.random.randint(jax.random.fold_in(key, 43), (NFAR,), 1, NCL)
    target = (anchor + offset) % NCL
    return (anchor.astype(jnp.int32), target.astype(jnp.int32))


def draw_far_src(key, part):
    return far_pairs(key)[0]


def draw_far_tgt(key, part):
    return far_pairs(key)[1]


def levels(rng, shape, pieces, low, high):
    def one(dim, parts):
        heights = jax.random.uniform(jax.random.fold_in(jax.random.fold_in(rng, 6), dim), (parts,), jnp.float32, low / len(pieces), high / len(pieces))
        return jnp.repeat(jnp.exp(heights), shape[dim] // parts).reshape((-1,) + (1,) * (len(shape) - dim - 1))

    loudness = one(*pieces[0])
    for cut in pieces[1:]:
        loudness = loudness * one(*cut)
    return loudness


def bell_draw(stream_key, extent, deviation, most, pieces=(), dtype=jnp.bfloat16):
    loudness = levels(stream_key, extent, pieces, -0.22, 0.18) if pieces else 1.0
    values = jax.random.normal(stream_key, extent, jnp.float32) * deviation * loudness
    return jnp.minimum(jnp.maximum(values, -most), most).astype(dtype)


def setup_inputs(seed: int = 0, part: int = 0) -> dict:
    streams_of = jax.random.split(jax.random.key(seed), 10)
    own_keys = jax.random.split(jax.random.fold_in(streams_of[9], part), 10)
    rhs_field = bell_draw(own_keys[0], (RHS, PANELS), 1.0, 6.0, ((0, 2), (1, 4)), jnp.float32)
    coefficients = jnp.clip(jax.random.uniform(streams_of[1], (DEG + 1,), jnp.float32, -1.0, 1.0), -1.0, 1.0)
    near_blocks = bell_draw(own_keys[2], (NNEAR, LEAF, LEAF), (2 * LEAF * NEAR_PER) ** -0.5, 0.125, ((0, 8),))
    near_tgt = draw_near_tgt(jax.random.fold_in(jax.random.fold_in(streams_of[9], part), 71), part)
    near_src = draw_near_src(jax.random.fold_in(jax.random.fold_in(streams_of[9], part), 71), part)
    row_basis = bell_draw(own_keys[5], (NCL, R, LEAF), (2 * R * FAR_PER) ** -0.5, 0.25, ((0, 4),))
    col_basis = bell_draw(own_keys[6], (NFAR, R, LEAF), LEAF ** -0.5, 0.375, ((0, 8),))
    far_src = draw_far_src(jax.random.fold_in(jax.random.fold_in(streams_of[9], part), 71), part)
    far_tgt = draw_far_tgt(jax.random.fold_in(jax.random.fold_in(streams_of[9], part), 71), part)
    return dict(rhs_field=rhs_field, coefficients=coefficients, near_blocks=near_blocks, near_tgt=near_tgt, near_src=near_src, row_basis=row_basis, col_basis=col_basis, far_src=far_src, far_tgt=far_tgt)


def reference(rhs_field, coefficients, near_blocks, near_tgt, near_src, row_basis, col_basis, far_src, far_tgt):
    source = rhs_field.reshape(RHS, NCL, LEAF)
    iterate = (coefficients[DEG] * source).astype(jnp.bfloat16)
    groups_count = NNEAR // NB_DEV
    blocks = near_blocks.reshape(groups_count, NB_DEV, LEAF, LEAF)
    targets = near_tgt.reshape(groups_count, NB_DEV).astype(jnp.int32)
    anchors = near_src.reshape(groups_count, NB_DEV).astype(jnp.int32)
    result = source
    for step in range(DEG):
        degree = DEG - 1 - step
        current = iterate

        def near_step(total, item):
            block_set, target_set, anchor_set = item
            gathered = current[:, anchor_set, :].astype(jnp.float32)
            partial_value = jnp.einsum("rjs,jts->rjt", gathered, block_set.astype(jnp.float32), precision=lax.Precision.HIGHEST)
            return total.at[:, target_set, :].add(partial_value), None

        near, unused = lax.scan(near_step, jnp.zeros((RHS, NCL, LEAF), jnp.float32), (blocks, targets, anchors))
        far_input = current[:, far_src, :].astype(jnp.float32)
        coef = jnp.einsum("rjl,jkl->rjk", far_input, col_basis.astype(jnp.float32), precision=lax.Precision.HIGHEST)
        sums = jnp.zeros((RHS, NCL, R), jnp.float32).at[:, far_tgt, :].add(coef)
        far = jnp.einsum("rck,ckl->rcl", sums, row_basis.astype(jnp.float32), precision=lax.Precision.HIGHEST)
        result = near + far + coefficients[degree] * source
        iterate = result.astype(jnp.bfloat16)
    return result.reshape(RHS, PANELS)
```

```python
import functools

import jax
import jax.numpy as jnp
from jax import lax
from jax.experimental import pallas as pl
from jax.experimental.pallas import tpu as pltpu
from jax.sharding import PartitionSpec as P

MESH = pl.DeviceIdType.MESH
F32 = jnp.float32
BF16 = jnp.bfloat16
CAP = 2
LANES = 128


def drain(buffer, sem):
    pltpu.make_async_copy(buffer, buffer, sem).wait()


def split(value):
    high = value.astype(BF16)
    return high, (value - high.astype(F32)).astype(BF16)


def kernel(
    sizes, coeff, near_tgt, near_src, far_src, far_tgt, rhs, near_hbm, row_hbm, col_hbm, out,
    near_v, row_v, col_v, xs, x0_send, x0_recv, x0_wide, u_recv, rq_send, rq_recv,
    src_lane, fold, s_send, s_recv, sums_v, n_send, n_recv, sel_send, sel_recv, index_s,
    load_sem, x0_sems, u_sems, rq_sems, s_sems, n_sems, sel_sems,
):
    clus, pairs, clusters, rows, leaf, rank, near_count, far_count, degree_top = sizes
    group = clus * pairs
    c = lax.axis_index("clus")
    p = lax.axis_index("pair")
    me = c * pairs + p
    up = lax.rem(c + 1, clus)
    down = lax.rem(c + clus - 1, clus)
    base = c * clusters
    beside = (down, up)

    loads = [
        pltpu.make_async_copy(src, dst, load_sem.at[i])
        for i, (src, dst) in enumerate(((col_hbm, col_v), (row_hbm, row_v), (near_hbm, near_v)))
    ]
    for load in loads:
        load.start()

    def each(first, count, body):
        if count - first <= 8:
            for i in range(first, count):
                body(i)
        else:
            lax.fori_loop(first, count, lambda i, x: (body(i), x)[1], 0)

    def peer(d):
        other = lax.rem(me + d, group)
        return {"clus": lax.div(other, pairs), "pair": lax.rem(other, pairs)}

    barrier = pltpu.get_barrier_semaphore()
    each(1, group, lambda d: pl.semaphore_signal(barrier, inc=1, device_id=peer(d), device_id_type=MESH))

    scale = coeff[degree_top]
    first = [(scale * rhs[:, s * leaf : (s + 1) * leaf]).astype(BF16).astype(F32) for s in range(clusters)]
    for s in range(clusters):
        xs[s] = first[s]
    x0_send[...] = jnp.concatenate(first, axis=0).astype(BF16)

    counts = [jnp.int32(0), jnp.int32(0)]
    wanted = [[jnp.int32(0)] * CAP, [jnp.int32(0)] * CAP]
    for j in range(near_count):
        owner = lax.div(near_src[j], clusters)
        local = near_src[j] - owner * clusters
        place = local
        for d in range(2):
            here = owner == beside[d]
            for u in range(CAP):
                wanted[d][u] = jnp.where(here & (counts[d] == u), local, wanted[d][u])
            place = jnp.where(here, clusters + d * CAP + jnp.minimum(counts[d], CAP - 1), place)
            counts[d] = counts[d] + jnp.where(here, 1, 0)
        index_s[j] = place
    cluster_row = lax.broadcasted_iota(jnp.int32, (clusters, LANES), 0)
    for d in range(2):
        for u in range(CAP):
            rq_send[d, u * clusters : (u + 1) * clusters, :] = jnp.where(cluster_row == wanted[d][u], 1.0, 0.0)

    pl.semaphore_wait(barrier, group - 1)

    def send(src, dst, send_sem, recv_sem, device):
        pltpu.make_async_remote_copy(
            src_ref=src, dst_ref=dst, send_sem=send_sem, recv_sem=recv_sem,
            device_id=device, device_id_type=MESH,
        ).start()

    for d in range(2):
        send(x0_send, x0_recv.at[1 - d], x0_sems.at[0, d], x0_sems.at[1, 1 - d], {"clus": beside[d], "pair": p})
    for d in range(2):
        def ask(e, d=d):
            device = {"clus": beside[d], "pair": lax.rem(p + e, pairs)}
            send(rq_send.at[d], rq_recv.at[1 - d, e], rq_sems.at[0, d], rq_sems.at[1, 1 - d], device)
        each(0, pairs, ask)
    loads[1].wait()
    for d in range(2):
        send(row_v, u_recv.at[1 - d], u_sems.at[0, d], u_sems.at[1, 1 - d], {"clus": beside[d], "pair": p})

    lane = lax.broadcasted_iota(jnp.int32, (rows, LANES), 1)
    per_tile = LANES // rank
    tiles = far_count // per_tile
    for q in range(tiles):
        value = jnp.zeros((rows, LANES), jnp.int32)
        for i in range(per_tile):
            value = jnp.where(lane >= i * rank, far_src[q * per_tile + i] - base, value)
        src_lane[:, q * LANES : (q + 1) * LANES] = value
    width = clus * clusters * rank
    offset = lax.broadcasted_iota(jnp.int32, (rank, width), 1) - lax.broadcasted_iota(jnp.int32, (rank, width), 0)

    def place_block(j, unused):
        start = pl.multiple_of(j * rank, rank)
        fold[pl.ds(start, rank), :] = jnp.where(offset == far_tgt[j] * rank, 1.0, 0.0).astype(BF16)
        return unused

    lax.fori_loop(0, far_count, place_block, 0, unroll=4)
    loads[0].wait()

    def far_mask(value, local):
        low = local * rank
        return jnp.where((lane >= low) & (lane < low + rank), value, 0.0)

    contract_last = (((1,), (1,)), ((), ()))
    for step in range(degree_top):
        degree = degree_top - 1 - step
        last = step == degree_top - 1

        own = jnp.concatenate([xs[s] for s in range(clusters)], axis=0).astype(BF16)
        every = lax.dot_general(own, col_v[...], contract_last, preferred_element_type=F32)
        coef = jnp.zeros((rows, far_count * rank), F32)
        source_of = src_lane[...]
        for s in range(clusters):
            coef = coef + jnp.where(source_of == s, every[s * rows : (s + 1) * rows], 0.0)
        both = jnp.dot(jnp.concatenate(split(coef), axis=0), fold[...], preferred_element_type=F32)
        mine = both[:rows] + both[rows:]
        chunk = clusters * rank
        mine = jnp.concatenate([mine[:, i * chunk : (i + 1) * chunk] for i in range(clus)], axis=0)
        s_send[step] = mine.astype(BF16)
        each(1, group, lambda d: send(
            s_send.at[step], s_recv.at[step, d - 1], s_sems.at[0, step], s_sems.at[1, step], peer(d)))

        if step == 0:
            for d in range(2):
                drain(x0_recv.at[d], x0_sems.at[1, d])
                wide = x0_recv[d].astype(F32)
                for s in range(clusters):
                    x0_wide[d, s] = wide[s * rows : (s + 1) * rows]
                for u in range(CAP):
                    xs[clusters + d * CAP + u] = x0_wide[d, wanted[d][u]]
            loads[2].wait()

        near = [jnp.zeros((rows, leaf), F32) for s in range(clusters)]
        for j in range(near_count):
            value = lax.dot_general(
                xs[index_s[j]].astype(BF16), near_v[j], contract_last, preferred_element_type=F32)
            target = near_tgt[j] - base
            for s in range(clusters):
                near[s] = near[s] + value * jnp.where(target == s, 1.0, 0.0)
        n_send[step] = jnp.concatenate(near, axis=0).astype(BF16)

        def share(e):
            send(n_send.at[step], n_recv.at[step, e - 1], n_sems.at[0, step], n_sems.at[1, step],
                 {"clus": c, "pair": lax.rem(p + e, pairs)})

        each(1, pairs, share)
        scaled = [coeff[degree] * rhs[:, s * leaf : (s + 1) * leaf] for s in range(clusters)]
        if not last:
            if step == 0:
                for d in range(2):
                    drain(rq_recv.at[d], rq_sems.at[1, d])
            leads = jnp.where(p == 0, 1.0, 0.0)
            with_rhs = [near[s] + leads * scaled[s] for s in range(clusters)]
            for d in range(2):
                for e in range(pairs):
                    parts = []
                    for u in range(CAP):
                        total = jnp.zeros((rows, leaf), F32)
                        for s in range(clusters):
                            weight = rq_recv[d, e, u * clusters + s : u * clusters + s + 1, :]
                            weight = jnp.concatenate([weight] * (leaf // LANES), axis=1)
                            total = total + weight * with_rhs[s]
                        parts.append(total)
                    sel_send[step, d, e] = jnp.concatenate(parts, axis=0).astype(BF16)
                    device = {"clus": beside[d], "pair": lax.rem(p + pairs - e, pairs)}
                    send(sel_send.at[step, d, e], sel_recv.at[step, 1 - d, e],
                         sel_sems.at[0, step, d], sel_sems.at[1, step, 1 - d], device)

        drain(s_recv.at[step], s_sems.at[1, step])
        if group <= 16:
            total = mine
            for d in range(group - 1):
                total = total + s_recv[step, d].astype(F32)
        else:
            total = lax.fori_loop(0, group - 1, lambda d, t: t + s_recv[step, d].astype(F32), mine)
        for i in range(clus):
            sums_v[i] = total[i * rows : (i + 1) * rows]
        masked = jnp.concatenate([far_mask(sums_v[c], s) for s in range(clusters)], axis=0)
        high, low = split(masked)
        far = jnp.dot(high, row_v[...], preferred_element_type=F32) + jnp.dot(low, row_v[...], preferred_element_type=F32)
        if not last:
            for d in range(2):
                if step == 0:
                    drain(u_recv.at[d], u_sems.at[1, d])
                around = sums_v[beside[d]]
                masked = jnp.concatenate([far_mask(around, wanted[d][u]) for u in range(CAP)], axis=0)
                high, low = split(masked)
                basis = u_recv[d]
                value = jnp.dot(high, basis, preferred_element_type=F32) + jnp.dot(low, basis, preferred_element_type=F32)
                drain(sel_recv.at[step, d], sel_sems.at[1, step, d])
                for e in range(pairs):
                    value = value + sel_recv[step, d, e].astype(F32)
                for u in range(CAP):
                    xs[clusters + d * CAP + u] = value[u * rows : (u + 1) * rows].astype(BF16).astype(F32)
        drain(n_recv.at[step], n_sems.at[1, step])
        total = far + jnp.concatenate(near, axis=0)
        for e in range(pairs - 1):
            total = total + n_recv[step, e].astype(F32)
        for s in range(clusters):
            result = total[s * rows : (s + 1) * rows] + scaled[s]
            if last:
                out[:, s * leaf : (s + 1) * leaf] = result
            else:
                xs[s] = result.astype(BF16).astype(F32)

    for d in range(2):
        drain(x0_send, x0_sems.at[0, d])
        drain(row_v, u_sems.at[0, d])
        drain(rq_recv.at[d], rq_sems.at[0, d])
    for step in range(degree_top):
        drain(s_recv.at[step], s_sems.at[0, step])
        drain(n_recv.at[step], n_sems.at[0, step])
        if step < degree_top - 1:
            for d in range(2):
                drain(sel_send.at[step, d], sel_sems.at[0, step, d])


def shards(
    clus, pairs, rhs_field, coefficients, near_blocks, near_tgt, near_src, row_basis, col_basis, far_src, far_tgt
):
    rows = rhs_field.shape[0]
    clusters, rank, leaf = row_basis.shape
    near_count, far_count = near_blocks.shape[0], col_basis.shape[0]
    degree_top = coefficients.shape[0] - 1
    group = clus * pairs
    chunk = clusters * rank
    sizes = (clus, pairs, clusters, rows, leaf, rank, near_count, far_count, degree_top)
    smem = pl.BlockSpec(memory_space=pltpu.SMEM)
    vmem = pl.BlockSpec(memory_space=pltpu.VMEM)
    hbm = pl.BlockSpec(memory_space=pl.ANY)
    fields = clusters * rows
    rounds = degree_top
    return pl.pallas_call(
        functools.partial(kernel, sizes),
        out_shape=jax.ShapeDtypeStruct(rhs_field.shape, F32),
        in_specs=[smem] * 5 + [vmem] + [hbm] * 3,
        out_specs=vmem,
        scratch_shapes=[
            pltpu.VMEM(near_blocks.shape, BF16),
            pltpu.VMEM((chunk, leaf), BF16),
            pltpu.VMEM((far_count * rank, leaf), BF16),
            pltpu.VMEM((clusters + 2 * CAP, rows, leaf), F32),
            pltpu.VMEM((fields, leaf), BF16),
            pltpu.VMEM((2, fields, leaf), BF16),
            pltpu.VMEM((2, clusters, rows, leaf), F32),
            pltpu.VMEM((2, chunk, leaf), BF16),
            pltpu.VMEM((2, CAP * clusters, LANES), F32),
            pltpu.VMEM((2, pairs, CAP * clusters, LANES), F32),
            pltpu.VMEM((rows, far_count * rank), jnp.int32),
            pltpu.VMEM((far_count * rank, clus * chunk), BF16),
            pltpu.VMEM((rounds, clus * rows, chunk), BF16),
            pltpu.VMEM((rounds, group - 1, clus * rows, chunk), BF16),
            pltpu.VMEM((clus, rows, chunk), F32),
            pltpu.VMEM((rounds, fields, leaf), BF16),
            pltpu.VMEM((rounds, pairs - 1, fields, leaf), BF16),
            pltpu.VMEM((rounds - 1, 2, pairs, CAP * rows, leaf), BF16),
            pltpu.VMEM((rounds - 1, 2, pairs, CAP * rows, leaf), BF16),
            pltpu.SMEM((near_count,), jnp.int32),
            pltpu.SemaphoreType.DMA((3,)),
            pltpu.SemaphoreType.DMA((2, 2)),
            pltpu.SemaphoreType.DMA((2, 2)),
            pltpu.SemaphoreType.DMA((2, 2)),
            pltpu.SemaphoreType.DMA((2, rounds)),
            pltpu.SemaphoreType.DMA((2, rounds)),
            pltpu.SemaphoreType.DMA((2, rounds - 1, 2)),
        ],
        compiler_params=pltpu.CompilerParams(
            collective_id=0, has_side_effects=True, vmem_limit_bytes=44 * 1024 * 1024
        ),
        name="horner",
    )(
        coefficients, near_tgt, near_src, far_src, far_tgt, rhs_field,
        near_blocks, row_basis.reshape(chunk, leaf), col_basis.reshape(far_count * rank, leaf),
    )


def solution(mesh):
    return jax.shard_map(
        functools.partial(shards, mesh.shape["clus"], mesh.shape["pair"]),
        mesh=mesh,
        in_specs=(
            P("rhs", ("groups", "clus")),
            P(),
            P(("groups", "clus", "pair"), None, None),
            P(("groups", "clus", "pair")),
            P(("groups", "clus", "pair")),
            P(("groups", "clus"), None, None),
            P(("groups", "clus", "pair"), None, None),
            P(("groups", "clus", "pair")),
            P(("groups", "clus", "pair")),
        ),
        out_specs=P("rhs", ("groups", "clus")),
        check_vma=False,
    )
```

```python
import functools

import jax
import jax.numpy as jnp
from jax import lax
from jax.experimental import pallas as pl
from jax.experimental.pallas import tpu as pltpu
from jax.sharding import PartitionSpec as P

MESH = pl.DeviceIdType.MESH
F32 = jnp.float32
BF16 = jnp.bfloat16
CAP = 2
LANES = 128


def drain(buffer, sem):
    pltpu.make_async_copy(buffer, buffer, sem).wait()


def split(value):
    high = value.astype(BF16)
    return high, (value - high.astype(F32)).astype(BF16)


def kernel(
    sizes, coeff_h, near_tgt_h, near_src_h, far_src_h, far_tgt_h, rhs_h, near_h, row_h, col_h, out,
    coeff, near_tgt, near_src, far_src, far_tgt, rhs, near_v, row_v, col_v,
    xs, x0_send, x0_recv, x0_wide, rq_send, rq_recv,
    src_lane, fold, s_send, s_recv, n_send, n_recv, sel_send, sel_recv, index_s,
    load_sem, x0_sems, rq_sems, s_sems, n_sems, sel_sems,
):
    clus, pairs, clusters, rows, leaf, rank, near_count, far_count, degree_top = sizes
    group = clus * pairs
    chunk = clusters * rank
    c = lax.axis_index("clus")
    p = lax.axis_index("pair")
    me = c * pairs + p
    up = lax.rem(c + 1, clus)
    down = lax.rem(c + clus - 1, clus)
    base = c * clusters
    beside = (down, up)

    places = (
        (coeff_h, coeff), (rhs_h, rhs), (far_tgt_h, far_tgt), (far_src_h, far_src), (near_src_h, near_src),
        (near_tgt_h, near_tgt), (col_h, col_v), (row_h, row_v), (near_h, near_v),
    )
    loads = [pltpu.make_async_copy(src, dst, load_sem.at[i]) for i, (src, dst) in enumerate(places)]
    for load in loads:
        load.start()

    def each(first, count, body):
        if count - first <= 8:
            for i in range(first, count):
                body(i)
        else:
            lax.fori_loop(first, count, lambda i, x: (body(i), x)[1], 0)

    def peer(d):
        other = lax.rem(me + d, group)
        return {"clus": lax.div(other, pairs), "pair": lax.rem(other, pairs)}

    barrier = pltpu.get_barrier_semaphore()
    each(1, group, lambda d: pl.semaphore_signal(barrier, inc=1, device_id=peer(d), device_id_type=MESH))

    def send(src, dst, send_sem, recv_sem, device):
        pltpu.make_async_remote_copy(
            src_ref=src, dst_ref=dst, send_sem=send_sem, recv_sem=recv_sem,
            device_id=device, device_id_type=MESH,
        ).start()

    for load in loads[:6]:
        load.wait()

    scale = coeff[degree_top]
    first = [(scale * rhs[:, s * leaf : (s + 1) * leaf]).astype(BF16).astype(F32) for s in range(clusters)]
    for s in range(clusters):
        xs[s] = first[s]
    x0_send[...] = jnp.concatenate(first, axis=0).astype(BF16)

    counts = [jnp.int32(0), jnp.int32(0)]
    wanted = [[jnp.int32(0)] * CAP, [jnp.int32(0)] * CAP]
    for j in range(near_count):
        owner = lax.div(near_src[j], clusters)
        local = near_src[j] - owner * clusters
        place = local
        for d in range(2):
            here = owner == beside[d]
            for u in range(CAP):
                wanted[d][u] = jnp.where(here & (counts[d] == u), local, wanted[d][u])
            place = jnp.where(here, clusters + d * CAP + jnp.minimum(counts[d], CAP - 1), place)
            counts[d] = counts[d] + jnp.where(here, 1, 0)
        index_s[j] = place
    cluster_row = lax.broadcasted_iota(jnp.int32, (clusters, LANES), 0)
    for d in range(2):
        for u in range(CAP):
            rq_send[d, u * clusters : (u + 1) * clusters, :] = jnp.where(cluster_row == wanted[d][u], 1.0, 0.0)

    pl.semaphore_wait(barrier, group - 1)
    for d in range(2):
        send(x0_send, x0_recv.at[1 - d], x0_sems.at[0, d], x0_sems.at[1, 1 - d], {"clus": beside[d], "pair": p})
    for d in range(2):
        def ask(e, d=d):
            device = {"clus": beside[d], "pair": lax.rem(p + e, pairs)}
            send(rq_send.at[d], rq_recv.at[1 - d, e], rq_sems.at[0, d], rq_sems.at[1, 1 - d], device)
        each(0, pairs, ask)

    lane = lax.broadcasted_iota(jnp.int32, (rows, LANES), 1)
    per_tile = LANES // rank
    for q in range(far_count // per_tile):
        value = jnp.zeros((rows, LANES), jnp.int32)
        for i in range(per_tile):
            value = jnp.where(lane >= i * rank, far_src[q * per_tile + i] - base, value)
        src_lane[:, q * LANES : (q + 1) * LANES] = value
    width = clus * chunk
    offset = lax.broadcasted_iota(jnp.int32, (rank, width), 1) - lax.broadcasted_iota(jnp.int32, (rank, width), 0)

    def place_block(j, unused):
        start = pl.multiple_of(j * rank, rank)
        fold[pl.ds(start, rank), :] = jnp.where(offset == far_tgt[j] * rank, 1.0, 0.0).astype(BF16)
        return unused

    lax.fori_loop(0, far_count, place_block, 0, unroll=4)
    loads[6].wait()
    loads[7].wait()

    contract_last = (((1,), (1,)), ((), ()))
    for step in range(degree_top):
        degree = degree_top - 1 - step
        last = step == degree_top - 1

        own = jnp.concatenate([xs[s] for s in range(clusters)], axis=0).astype(BF16)
        every = lax.dot_general(own, col_v[...], contract_last, preferred_element_type=F32)
        coef = jnp.zeros((rows, far_count * rank), F32)
        source_of = src_lane[...]
        for s in range(clusters):
            coef = coef + jnp.where(source_of == s, every[s * rows : (s + 1) * rows], 0.0)
        both = jnp.dot(jnp.concatenate(split(coef), axis=0), fold[...], preferred_element_type=F32)
        mine = both[:rows] + both[rows:]
        for i in range(clus):
            s_send[step, i] = mine[:, i * chunk : (i + 1) * chunk]

        def spread(d):
            there = lax.rem(c + d, clus)
            send(s_send.at[step, there], s_recv.at[step, d - 1], s_sems.at[0, step], s_sems.at[1, step],
                 {"clus": there, "pair": p})

        each(1, clus, spread)

        if step == 0:
            for d in range(2):
                drain(x0_recv.at[d], x0_sems.at[1, d])
                wide = x0_recv[d].astype(F32)
                for s in range(clusters):
                    x0_wide[d, s] = wide[s * rows : (s + 1) * rows]
                for u in range(CAP):
                    xs[clusters + d * CAP + u] = x0_wide[d, wanted[d][u]]
            loads[8].wait()
        else:
            for d in range(2):
                drain(sel_recv.at[step - 1, d], sel_sems.at[1, step - 1, d])
                value = sel_recv[step - 1, d, 0].astype(F32)
                for e in range(1, pairs):
                    value = value + sel_recv[step - 1, d, e].astype(F32)
                for u in range(CAP):
                    xs[clusters + d * CAP + u] = value[u * rows : (u + 1) * rows].astype(BF16).astype(F32)

        near = [jnp.zeros((rows, leaf), F32) for s in range(clusters)]
        for j in range(near_count):
            value = lax.dot_general(
                xs[index_s[j]].astype(BF16), near_v[j], contract_last, preferred_element_type=F32)
            target = near_tgt[j] - base
            for s in range(clusters):
                near[s] = near[s] + value * jnp.where(target == s, 1.0, 0.0)

        drain(s_recv.at[step], s_sems.at[1, step])
        sums = s_send[step, c]
        for d in range(clus - 1):
            sums = sums + s_recv[step, d]
        masked = jnp.concatenate(
            [jnp.where((lane >= s * rank) & (lane < (s + 1) * rank), sums, 0.0) for s in range(clusters)], axis=0)
        both = jnp.dot(jnp.concatenate(split(masked), axis=0), row_v[...], preferred_element_type=F32)
        part = both[: clusters * rows] + both[clusters * rows :] + jnp.concatenate(near, axis=0)
        n_send[step] = part.astype(BF16)

        def share(e):
            send(n_send.at[step], n_recv.at[step, e - 1], n_sems.at[0, step], n_sems.at[1, step],
                 {"clus": c, "pair": lax.rem(p + e, pairs)})

        each(1, pairs, share)
        scaled = jnp.concatenate([coeff[degree] * rhs[:, s * leaf : (s + 1) * leaf] for s in range(clusters)], axis=0)
        if not last:
            if step == 0:
                for d in range(2):
                    drain(rq_recv.at[d], rq_sems.at[1, d])
            with_rhs = part + jnp.where(p == 0, 1.0, 0.0) * scaled
            for d in range(2):
                for e in range(pairs):
                    parts = []
                    for u in range(CAP):
                        total = jnp.zeros((rows, leaf), F32)
                        for s in range(clusters):
                            weight = rq_recv[d, e, u * clusters + s : u * clusters + s + 1, :]
                            weight = jnp.concatenate([weight] * (leaf // LANES), axis=1)
                            total = total + weight * with_rhs[s * rows : (s + 1) * rows]
                        parts.append(total)
                    sel_send[step, d, e] = jnp.concatenate(parts, axis=0).astype(BF16)
                    device = {"clus": beside[d], "pair": lax.rem(p + pairs - e, pairs)}
                    send(sel_send.at[step, d, e], sel_recv.at[step, 1 - d, e],
                         sel_sems.at[0, step, d], sel_sems.at[1, step, 1 - d], device)

        total = part + scaled
        drain(n_recv.at[step], n_sems.at[1, step])
        for e in range(pairs - 1):
            total = total + n_recv[step, e].astype(F32)
        for s in range(clusters):
            result = total[s * rows : (s + 1) * rows]
            if last:
                out[:, s * leaf : (s + 1) * leaf] = result
            else:
                xs[s] = result.astype(BF16).astype(F32)

    for d in range(2):
        drain(x0_send, x0_sems.at[0, d])
        drain(rq_recv.at[d], rq_sems.at[0, d])
    for step in range(degree_top):
        drain(s_recv.at[step], s_sems.at[0, step])
        drain(n_recv.at[step], n_sems.at[0, step])
        if step < degree_top - 1:
            for d in range(2):
                drain(sel_send.at[step, d], sel_sems.at[0, step, d])


def shards(
    clus, pairs, rhs_field, coefficients, near_blocks, near_tgt, near_src, row_basis, col_basis, far_src, far_tgt
):
    rows = rhs_field.shape[0]
    clusters, rank, leaf = row_basis.shape
    near_count, far_count = near_blocks.shape[0], col_basis.shape[0]
    degree_top = coefficients.shape[0] - 1
    chunk = clusters * rank
    sizes = (clus, pairs, clusters, rows, leaf, rank, near_count, far_count, degree_top)
    hbm = pl.BlockSpec(memory_space=pltpu.HBM)
    fields = clusters * rows
    rounds = degree_top
    return pl.pallas_call(
        functools.partial(kernel, sizes),
        out_shape=jax.ShapeDtypeStruct(rhs_field.shape, F32),
        in_specs=[hbm] * 9,
        out_specs=pl.BlockSpec(memory_space=pltpu.VMEM),
        scratch_shapes=[
            pltpu.SMEM(coefficients.shape, F32),
            pltpu.SMEM(near_tgt.shape, jnp.int32),
            pltpu.SMEM(near_src.shape, jnp.int32),
            pltpu.SMEM(far_src.shape, jnp.int32),
            pltpu.SMEM(far_tgt.shape, jnp.int32),
            pltpu.VMEM(rhs_field.shape, F32),
            pltpu.VMEM(near_blocks.shape, BF16),
            pltpu.VMEM((chunk, leaf), BF16),
            pltpu.VMEM((far_count * rank, leaf), BF16),
            pltpu.VMEM((clusters + 2 * CAP, rows, leaf), F32),
            pltpu.VMEM((fields, leaf), BF16),
            pltpu.VMEM((2, fields, leaf), BF16),
            pltpu.VMEM((2, clusters, rows, leaf), F32),
            pltpu.VMEM((2, CAP * clusters, LANES), F32),
            pltpu.VMEM((2, pairs, CAP * clusters, LANES), F32),
            pltpu.VMEM((rows, far_count * rank), jnp.int32),
            pltpu.VMEM((far_count * rank, clus * chunk), BF16),
            pltpu.VMEM((rounds, clus, rows, chunk), F32),
            pltpu.VMEM((rounds, clus - 1, rows, chunk), F32),
            pltpu.VMEM((rounds, fields, leaf), BF16),
            pltpu.VMEM((rounds, pairs - 1, fields, leaf), BF16),
            pltpu.VMEM((rounds - 1, 2, pairs, CAP * rows, leaf), BF16),
            pltpu.VMEM((rounds - 1, 2, pairs, CAP * rows, leaf), BF16),
            pltpu.SMEM((near_count,), jnp.int32),
            pltpu.SemaphoreType.DMA((9,)),
            pltpu.SemaphoreType.DMA((2, 2)),
            pltpu.SemaphoreType.DMA((2, 2)),
            pltpu.SemaphoreType.DMA((2, rounds)),
            pltpu.SemaphoreType.DMA((2, rounds)),
            pltpu.SemaphoreType.DMA((2, rounds - 1, 2)),
        ],
        compiler_params=pltpu.CompilerParams(
            collective_id=0, has_side_effects=True, vmem_limit_bytes=44 * 1024 * 1024
        ),
        name="horner",
    )(
        coefficients, near_tgt, near_src, far_src, far_tgt, rhs_field,
        near_blocks, row_basis.reshape(chunk, leaf), col_basis.reshape(far_count * rank, leaf),
    )


def solution(mesh):
    return jax.shard_map(
        functools.partial(shards, mesh.shape["clus"], mesh.shape["pair"]),
        mesh=mesh,
        in_specs=(
            P("rhs", ("groups", "clus")),
            P(),
            P(("groups", "clus", "pair"), None, None),
            P(("groups", "clus", "pair")),
            P(("groups", "clus", "pair")),
            P(("groups", "clus"), None, None),
            P(("groups", "clus", "pair"), None, None),
            P(("groups", "clus", "pair")),
            P(("groups", "clus", "pair")),
        ),
        out_specs=P("rhs", ("groups", "clus")),
        check_vma=False,
    )
```

```python
import functools

import jax
import jax.numpy as jnp
from jax import lax
from jax.experimental import pallas as pl
from jax.experimental.pallas import tpu as pltpu
from jax.sharding import PartitionSpec as P

MESH = pl.DeviceIdType.MESH
F32 = jnp.float32
BF16 = jnp.bfloat16
CAP = 2
LANES = 128
NEAR_UNROLL = 4
WIRE = BF16


def drain(buffer, sem):
    pltpu.make_async_copy(buffer, buffer, sem).wait()


def split(value):
    high = value.astype(BF16)
    return high, (value - high.astype(F32)).astype(BF16)


def kernel(
    sizes, coeff_h, near_tgt_h, near_src_h, far_src_h, far_tgt_h, rhs_h, near_h, row_h, col_h, out,
    coeff, near_tgt, near_src, far_src, far_tgt, rhs, near_v, row_v, col_v,
    xs, x0_send, x0_recv, x0_wide, rq_send, rq_recv,
    src_lane, held, fold, s_send, s_recv, n_send, n_recv, sel_send, sel_recv, index_s,
    load_sem, x0_sems, rq_sems, s_sems, n_sems, sel_sems,
):
    clus, pairs, clusters, rows, leaf, rank, near_count, far_count, degree_top = sizes
    group = clus * pairs
    chunk = clusters * rank
    c = lax.axis_index("clus")
    p = lax.axis_index("pair")
    me = c * pairs + p
    up = lax.rem(c + 1, clus)
    down = lax.rem(c + clus - 1, clus)
    base = c * clusters
    beside = (down, up)

    places = (
        (coeff_h, coeff), (rhs_h, rhs), (far_tgt_h, far_tgt), (far_src_h, far_src), (near_src_h, near_src),
        (near_tgt_h, near_tgt), (col_h, col_v), (row_h, row_v), (near_h, near_v),
    )
    loads = [pltpu.make_async_copy(src, dst, load_sem.at[i]) for i, (src, dst) in enumerate(places)]
    for load in loads:
        load.start()

    def each(first, count, body):
        if count - first <= 2:
            for i in range(first, count):
                body(i)
        else:
            lax.fori_loop(first, count, lambda i, x: (body(i), x)[1], 0)

    def peer(d):
        other = lax.rem(me + d, group)
        return {"clus": lax.div(other, pairs), "pair": lax.rem(other, pairs)}

    barrier = pltpu.get_barrier_semaphore()
    each(1, group, lambda d: pl.semaphore_signal(barrier, inc=1, device_id=peer(d), device_id_type=MESH))

    def send(src, dst, send_sem, recv_sem, device):
        pltpu.make_async_remote_copy(
            src_ref=src, dst_ref=dst, send_sem=send_sem, recv_sem=recv_sem,
            device_id=device, device_id_type=MESH,
        ).start()

    for load in loads[:6]:
        load.wait()

    scale = coeff[degree_top]
    first = [(scale * rhs[:, s * leaf : (s + 1) * leaf]).astype(BF16).astype(F32) for s in range(clusters)]
    for s in range(clusters):
        xs[s] = first[s]
    x0_send[...] = jnp.concatenate(first, axis=0).astype(BF16)

    def find(j, state):
        counts, wanted = list(state[:2]), list(state[2:])
        owner = lax.div(near_src[j], clusters)
        local = near_src[j] - owner * clusters
        place = local
        for d in range(2):
            here = owner == beside[d]
            for u in range(CAP):
                wanted[d * CAP + u] = jnp.where(here & (counts[d] == u), local, wanted[d * CAP + u])
            place = jnp.where(here, clusters + d * CAP + jnp.minimum(counts[d], CAP - 1), place)
            counts[d] = counts[d] + jnp.where(here, 1, 0)
        index_s[j] = place
        return (*counts, *wanted)

    wanted = lax.fori_loop(0, near_count, find, (jnp.int32(0),) * (2 + 2 * CAP))[2:]
    cluster_row = lax.broadcasted_iota(jnp.int32, (clusters, LANES), 0)
    for d in range(2):
        for u in range(CAP):
            rq_send[d, u * clusters : (u + 1) * clusters, :] = jnp.where(cluster_row == wanted[d * CAP + u], 1.0, 0.0)

    pl.semaphore_wait(barrier, group - 1)
    for d in range(2):
        send(x0_send, x0_recv.at[1 - d], x0_sems.at[0, d], x0_sems.at[1, 1 - d], {"clus": beside[d], "pair": p})
    for d in range(2):
        def ask(e, d=d):
            device = {"clus": beside[d], "pair": lax.rem(p + e, pairs)}
            send(rq_send.at[d], rq_recv.at[1 - d, e], rq_sems.at[0, d], rq_sems.at[1, 1 - d], device)
        each(0, pairs, ask)

    lane = lax.broadcasted_iota(jnp.int32, (rows, LANES), 1)
    per_tile = LANES // rank

    def mark_tile(q, unused):
        value = jnp.zeros((rows, LANES), jnp.int32)
        for i in range(per_tile):
            value = jnp.where(lane >= i * rank, far_src[q * per_tile + i] - base, value)
        src_lane[q] = value
        return unused

    lax.fori_loop(0, far_count // per_tile, mark_tile, 0)
    width = clus * chunk
    offset = lax.broadcasted_iota(jnp.int32, (rank, width), 1) - lax.broadcasted_iota(jnp.int32, (rank, width), 0)

    def place_block(j, unused):
        start = pl.multiple_of(j * rank, rank)
        fold[pl.ds(start, rank), :] = jnp.where(offset == far_tgt[j] * rank, 1.0, 0.0).astype(BF16)
        return unused

    lax.fori_loop(0, far_count, place_block, 0, unroll=2)
    loads[6].wait()
    loads[7].wait()

    contract_last = (((1,), (1,)), ((), ()))
    tile_lanes = far_count // per_tile

    def product(step, unused):
        degree = degree_top - 1 - step

        own = jnp.concatenate([xs[s] for s in range(clusters)], axis=0).astype(BF16)
        every = lax.dot_general(own, col_v[...], contract_last, preferred_element_type=F32)
        parts = []
        for q in range(tile_lanes):
            source_of = src_lane[q]
            total = jnp.zeros((rows, LANES), F32)
            for s in range(clusters):
                piece = every[s * rows : (s + 1) * rows, q * LANES : (q + 1) * LANES]
                total = total + jnp.where(source_of == s, piece, 0.0)
            parts.append(total)
        coef = jnp.concatenate(parts, axis=1)
        both = jnp.dot(jnp.concatenate(split(coef), axis=0), fold[...], preferred_element_type=F32)
        mine = both[:rows] + both[rows:]
        for i in range(clus):
            s_send[step, i] = mine[:, i * chunk : (i + 1) * chunk]

        def spread(d):
            there = lax.rem(c + d, clus)
            send(s_send.at[step, there], s_recv.at[step, d - 1], s_sems.at[0, step], s_sems.at[1, step],
                 {"clus": there, "pair": p})

        each(1, clus, spread)

        @pl.when(step == 0)
        def _():
            for d in range(2):
                drain(x0_recv.at[d], x0_sems.at[1, d])
                wide = x0_recv[d].astype(F32)
                for s in range(clusters):
                    x0_wide[d, s] = wide[s * rows : (s + 1) * rows]
                for u in range(CAP):
                    xs[clusters + d * CAP + u] = x0_wide[d, wanted[d * CAP + u]]
            loads[8].wait()

        @pl.when(step > 0)
        def _():
            for d in range(2):
                drain(sel_recv.at[step - 1, d], sel_sems.at[1, step - 1, d])
                value = sel_recv[step - 1, d, 0].astype(F32)
                for e in range(1, pairs):
                    value = value + sel_recv[step - 1, d, e].astype(F32)
                for u in range(CAP):
                    xs[clusters + d * CAP + u] = value[u * rows : (u + 1) * rows].astype(BF16).astype(F32)

        def near_block(i, near):
            near = list(near)
            for k in range(NEAR_UNROLL):
                j = i * NEAR_UNROLL + k
                value = lax.dot_general(
                    xs[index_s[j]].astype(BF16), near_v[j], contract_last, preferred_element_type=F32)
                target = near_tgt[j] - base
                for s in range(clusters):
                    near[s] = near[s] + value * jnp.where(target == s, 1.0, 0.0)
            return tuple(near)

        near = lax.fori_loop(
            0, near_count // NEAR_UNROLL, near_block,
            tuple(jnp.zeros((rows, leaf), F32) for s in range(clusters)))

        drain(s_recv.at[step], s_sems.at[1, step])
        sums = s_send[step, c]
        for d in range(clus - 1):
            sums = sums + s_recv[step, d]
        masked = jnp.concatenate(
            [jnp.where((lane >= s * rank) & (lane < (s + 1) * rank), sums, 0.0) for s in range(clusters)], axis=0)
        both = jnp.dot(jnp.concatenate(split(masked), axis=0), row_v[...], preferred_element_type=F32)
        part = both[: clusters * rows] + both[clusters * rows :] + jnp.concatenate(near, axis=0)
        n_send[step] = part.astype(WIRE)

        def share(e):
            send(n_send.at[step], n_recv.at[step, e - 1], n_sems.at[0, step], n_sems.at[1, step],
                 {"clus": c, "pair": lax.rem(p + e, pairs)})

        each(1, pairs, share)
        scaled = jnp.concatenate([coeff[degree] * rhs[:, s * leaf : (s + 1) * leaf] for s in range(clusters)], axis=0)

        @pl.when(step < degree_top - 1)
        def _():
            @pl.when(step == 0)
            def _():
                for d in range(2):
                    drain(rq_recv.at[d], rq_sems.at[1, d])

            with_rhs = part + jnp.where(p == 0, 1.0, 0.0) * scaled
            for s in range(clusters):
                held[s] = with_rhs[s * rows : (s + 1) * rows]

            def answer(i):
                d = lax.div(i, pairs)
                e = lax.rem(i, pairs)
                parts = []
                for u in range(CAP):
                    total = jnp.zeros((rows, leaf), F32)
                    for s in range(clusters):
                        weight = rq_recv[d, e, u * clusters + s : u * clusters + s + 1, :]
                        weight = jnp.concatenate([weight] * (leaf // LANES), axis=1)
                        total = total + weight * held[s]
                    parts.append(total)
                sel_send[step, d, e] = jnp.concatenate(parts, axis=0).astype(WIRE)
                there = jnp.where(d == 0, down, up)
                device = {"clus": there, "pair": lax.rem(p + pairs - e, pairs)}
                send(sel_send.at[step, d, e], sel_recv.at[step, 1 - d, e],
                     sel_sems.at[0, step, d], sel_sems.at[1, step, 1 - d], device)

            each(0, 2 * pairs, answer)

        total = part + scaled
        drain(n_recv.at[step], n_sems.at[1, step])
        for e in range(pairs - 1):
            total = total + n_recv[step, e].astype(F32)
        for s in range(clusters):
            result = total[s * rows : (s + 1) * rows]
            out[:, s * leaf : (s + 1) * leaf] = result
            xs[s] = result.astype(BF16).astype(F32)
        return unused

    lax.fori_loop(0, degree_top, product, 0)

    for d in range(2):
        drain(x0_send, x0_sems.at[0, d])
        drain(rq_recv.at[d], rq_sems.at[0, d])
    for step in range(degree_top):
        drain(s_recv.at[step], s_sems.at[0, step])
        drain(n_recv.at[step], n_sems.at[0, step])
        if step < degree_top - 1:
            for d in range(2):
                drain(sel_send.at[step, d], sel_sems.at[0, step, d])


def shards(
    clus, pairs, rhs_field, coefficients, near_blocks, near_tgt, near_src, row_basis, col_basis, far_src, far_tgt
):
    rows = rhs_field.shape[0]
    clusters, rank, leaf = row_basis.shape
    near_count, far_count = near_blocks.shape[0], col_basis.shape[0]
    degree_top = coefficients.shape[0] - 1
    chunk = clusters * rank
    sizes = (clus, pairs, clusters, rows, leaf, rank, near_count, far_count, degree_top)
    hbm = pl.BlockSpec(memory_space=pltpu.HBM)
    fields = clusters * rows
    rounds = degree_top
    return pl.pallas_call(
        functools.partial(kernel, sizes),
        out_shape=jax.ShapeDtypeStruct(rhs_field.shape, F32),
        in_specs=[hbm] * 9,
        out_specs=pl.BlockSpec(memory_space=pltpu.VMEM),
        scratch_shapes=[
            pltpu.SMEM(coefficients.shape, F32),
            pltpu.SMEM(near_tgt.shape, jnp.int32),
            pltpu.SMEM(near_src.shape, jnp.int32),
            pltpu.SMEM(far_src.shape, jnp.int32),
            pltpu.SMEM(far_tgt.shape, jnp.int32),
            pltpu.VMEM(rhs_field.shape, F32),
            pltpu.VMEM(near_blocks.shape, BF16),
            pltpu.VMEM((chunk, leaf), BF16),
            pltpu.VMEM((far_count * rank, leaf), BF16),
            pltpu.VMEM((clusters + 2 * CAP, rows, leaf), F32),
            pltpu.VMEM((fields, leaf), BF16),
            pltpu.VMEM((2, fields, leaf), BF16),
            pltpu.VMEM((2, clusters, rows, leaf), F32),
            pltpu.VMEM((2, CAP * clusters, LANES), F32),
            pltpu.VMEM((2, pairs, CAP * clusters, LANES), F32),
            pltpu.VMEM((far_count * rank // LANES, rows, LANES), jnp.int32),
            pltpu.VMEM((clusters, rows, leaf), F32),
            pltpu.VMEM((far_count * rank, clus * chunk), BF16),
            pltpu.VMEM((rounds, clus, rows, chunk), F32),
            pltpu.VMEM((rounds, clus - 1, rows, chunk), F32),
            pltpu.VMEM((rounds, fields, leaf), WIRE),
            pltpu.VMEM((rounds, pairs - 1, fields, leaf), WIRE),
            pltpu.VMEM((rounds - 1, 2, pairs, CAP * rows, leaf), WIRE),
            pltpu.VMEM((rounds - 1, 2, pairs, CAP * rows, leaf), WIRE),
            pltpu.SMEM((near_count,), jnp.int32),
            pltpu.SemaphoreType.DMA((9,)),
            pltpu.SemaphoreType.DMA((2, 2)),
            pltpu.SemaphoreType.DMA((2, 2)),
            pltpu.SemaphoreType.DMA((2, rounds)),
            pltpu.SemaphoreType.DMA((2, rounds)),
            pltpu.SemaphoreType.DMA((2, rounds - 1, 2)),
        ],
        compiler_params=pltpu.CompilerParams(
            collective_id=0, has_side_effects=True, vmem_limit_bytes=63 * 1024 * 1024
        ),
        name="horner",
    )(
        coefficients, near_tgt, near_src, far_src, far_tgt, rhs_field,
        near_blocks, row_basis.reshape(chunk, leaf), col_basis.reshape(far_count * rank, leaf),
    )


def solution(mesh):
    return jax.shard_map(
        functools.partial(shards, mesh.shape["clus"], mesh.shape["pair"]),
        mesh=mesh,
        in_specs=(
            P("rhs", ("groups", "clus")),
            P(),
            P(("groups", "clus", "pair"), None, None),
            P(("groups", "clus", "pair")),
            P(("groups", "clus", "pair")),
            P(("groups", "clus"), None, None),
            P(("groups", "clus", "pair"), None, None),
            P(("groups", "clus", "pair")),
            P(("groups", "clus", "pair")),
        ),
        out_specs=P("rhs", ("groups", "clus")),
        check_vma=False,
    )
```

```python
import functools

import jax
import jax.numpy as jnp
from jax import lax
from jax.experimental import pallas as pl
from jax.experimental.pallas import tpu as pltpu
from jax.sharding import PartitionSpec as P

MESH = pl.DeviceIdType.MESH
F32 = jnp.float32
BF16 = jnp.bfloat16
CAP = 2
LANES = 128
NEAR_UNROLL = 4
WIRE = BF16


def drain(buffer, sem):
    pltpu.make_async_copy(buffer, buffer, sem).wait()


def split(value):
    high = value.astype(BF16)
    return high, (value - high.astype(F32)).astype(BF16)


def kernel(
    sizes, coeff_h, near_tgt_h, near_src_h, far_src_h, far_tgt_h, rhs_h, near_h, row_h, col_h, out,
    coeff, near_tgt, near_src, far_src, far_tgt, rhs, near_v, row_v, col_v,
    xs, x0_send, x0_recv, x0_wide, rq_send, rq_recv,
    u_recv, far_side, src_lane, held, fold, s_send, s_recv, n_send, n_recv, sel_send, sel_recv, index_s,
    load_sem, x0_sems, u_sems, rq_sems, s_sems, n_sems, sel_sems,
):
    clus, pairs, clusters, rows, leaf, rank, near_count, far_count, degree_top = sizes
    group = clus * pairs
    chunk = clusters * rank
    c = lax.axis_index("clus")
    p = lax.axis_index("pair")
    me = c * pairs + p
    up = lax.rem(c + 1, clus)
    down = lax.rem(c + clus - 1, clus)
    base = c * clusters
    beside = (down, up)

    places = (
        (coeff_h, coeff), (rhs_h, rhs), (far_tgt_h, far_tgt), (far_src_h, far_src), (near_src_h, near_src),
        (near_tgt_h, near_tgt), (col_h, col_v), (row_h, row_v), (near_h, near_v),
    )
    loads = [pltpu.make_async_copy(src, dst, load_sem.at[i]) for i, (src, dst) in enumerate(places)]
    for load in loads:
        load.start()

    def each(first, count, body):
        if count - first <= 2:
            for i in range(first, count):
                body(i)
        else:
            lax.fori_loop(first, count, lambda i, x: (body(i), x)[1], 0)

    def peer(d):
        other = lax.rem(me + d, group)
        return {"clus": lax.div(other, pairs), "pair": lax.rem(other, pairs)}

    barrier = pltpu.get_barrier_semaphore()
    each(1, group, lambda d: pl.semaphore_signal(barrier, inc=1, device_id=peer(d), device_id_type=MESH))

    def send(src, dst, send_sem, recv_sem, device):
        pltpu.make_async_remote_copy(
            src_ref=src, dst_ref=dst, send_sem=send_sem, recv_sem=recv_sem,
            device_id=device, device_id_type=MESH,
        ).start()

    for load in loads[:6]:
        load.wait()

    scale = coeff[degree_top]
    first = [(scale * rhs[:, s * leaf : (s + 1) * leaf]).astype(BF16).astype(F32) for s in range(clusters)]
    for s in range(clusters):
        xs[s] = first[s]
    x0_send[...] = jnp.concatenate(first, axis=0).astype(BF16)

    def find(j, state):
        counts, wanted = list(state[:2]), list(state[2:])
        owner = lax.div(near_src[j], clusters)
        local = near_src[j] - owner * clusters
        place = local
        for d in range(2):
            here = owner == beside[d]
            for u in range(CAP):
                wanted[d * CAP + u] = jnp.where(here & (counts[d] == u), local, wanted[d * CAP + u])
            place = jnp.where(here, clusters + d * CAP + jnp.minimum(counts[d], CAP - 1), place)
            counts[d] = counts[d] + jnp.where(here, 1, 0)
        index_s[j] = place
        return (*counts, *wanted)

    wanted = lax.fori_loop(0, near_count, find, (jnp.int32(0),) * (2 + 2 * CAP))[2:]
    cluster_row = lax.broadcasted_iota(jnp.int32, (clusters, LANES), 0)
    for d in range(2):
        for u in range(CAP):
            rq_send[d, u * clusters : (u + 1) * clusters, :] = jnp.where(cluster_row == wanted[d * CAP + u], 1.0, 0.0)

    pl.semaphore_wait(barrier, group - 1)
    for d in range(2):
        send(x0_send, x0_recv.at[1 - d], x0_sems.at[0, d], x0_sems.at[1, 1 - d], {"clus": beside[d], "pair": p})
    for d in range(2):
        def ask(e, d=d):
            device = {"clus": beside[d], "pair": lax.rem(p + e, pairs)}
            send(rq_send.at[d], rq_recv.at[1 - d, e], rq_sems.at[0, d], rq_sems.at[1, 1 - d], device)
        each(0, pairs, ask)
    loads[7].wait()
    for d in range(2):
        send(row_v, u_recv.at[1 - d], u_sems.at[0, d], u_sems.at[1, 1 - d], {"clus": beside[d], "pair": p})

    lane = lax.broadcasted_iota(jnp.int32, (rows, LANES), 1)
    per_tile = LANES // rank

    def mark_tile(q, unused):
        value = jnp.zeros((rows, LANES), jnp.int32)
        for i in range(per_tile):
            value = jnp.where(lane >= i * rank, far_src[q * per_tile + i] - base, value)
        src_lane[q] = value
        return unused

    lax.fori_loop(0, far_count // per_tile, mark_tile, 0)
    width = clus * chunk
    offset = lax.broadcasted_iota(jnp.int32, (rank, width), 1) - lax.broadcasted_iota(jnp.int32, (rank, width), 0)

    def place_block(j, unused):
        start = pl.multiple_of(j * rank, rank)
        fold[pl.ds(start, rank), :] = jnp.where(offset == far_tgt[j] * rank, 1.0, 0.0).astype(BF16)
        return unused

    lax.fori_loop(0, far_count, place_block, 0, unroll=2)
    loads[6].wait()

    contract_last = (((1,), (1,)), ((), ()))
    tile_lanes = far_count // per_tile

    def product(step, unused):
        degree = degree_top - 1 - step

        own = jnp.concatenate([xs[s] for s in range(clusters)], axis=0).astype(BF16)
        every = lax.dot_general(own, col_v[...], contract_last, preferred_element_type=F32)
        parts = []
        for q in range(tile_lanes):
            source_of = src_lane[q]
            total = jnp.zeros((rows, LANES), F32)
            for s in range(clusters):
                piece = every[s * rows : (s + 1) * rows, q * LANES : (q + 1) * LANES]
                total = total + jnp.where(source_of == s, piece, 0.0)
            parts.append(total)
        coef = jnp.concatenate(parts, axis=1)
        both = jnp.dot(jnp.concatenate(split(coef), axis=0), fold[...], preferred_element_type=F32)
        mine = both[:rows] + both[rows:]
        chunks = [mine[:, i * chunk : (i + 1) * chunk] for i in range(clus)]
        for i in range(clus):
            s_send[step, i] = jnp.concatenate([chunks[(i + k) % clus] for k in (-1, 0, 1)], axis=0)

        def spread(d):
            device = peer(d)
            send(s_send.at[step, device["clus"]], s_recv.at[step, d - 1], s_sems.at[0, step], s_sems.at[1, step], device)

        each(1, group, spread)

        @pl.when(step == 0)
        def _():
            for d in range(2):
                drain(x0_recv.at[d], x0_sems.at[1, d])
                wide = x0_recv[d].astype(F32)
                for s in range(clusters):
                    x0_wide[d, s] = wide[s * rows : (s + 1) * rows]
                for u in range(CAP):
                    xs[clusters + d * CAP + u] = x0_wide[d, wanted[d * CAP + u]]
            loads[8].wait()

        @pl.when(step > 0)
        def _():
            for d in range(2):
                drain(sel_recv.at[step - 1, d], sel_sems.at[1, step - 1, d])
                value = far_side[d]
                for e in range(pairs):
                    value = value + sel_recv[step - 1, d, e].astype(F32)
                for u in range(CAP):
                    xs[clusters + d * CAP + u] = value[u * rows : (u + 1) * rows].astype(BF16).astype(F32)

        def near_block(i, near):
            near = list(near)
            for k in range(NEAR_UNROLL):
                j = i * NEAR_UNROLL + k
                value = lax.dot_general(
                    xs[index_s[j]].astype(BF16), near_v[j], contract_last, preferred_element_type=F32)
                target = near_tgt[j] - base
                for s in range(clusters):
                    near[s] = near[s] + value * jnp.where(target == s, 1.0, 0.0)
            return tuple(near)

        near = lax.fori_loop(
            0, near_count // NEAR_UNROLL, near_block,
            tuple(jnp.zeros((rows, leaf), F32) for s in range(clusters)))

        part = jnp.concatenate(near, axis=0)
        n_send[step] = part.astype(WIRE)

        def share(e):
            send(n_send.at[step], n_recv.at[step, e - 1], n_sems.at[0, step], n_sems.at[1, step],
                 {"clus": c, "pair": lax.rem(p + e, pairs)})

        each(1, pairs, share)
        scaled = jnp.concatenate([coeff[degree] * rhs[:, s * leaf : (s + 1) * leaf] for s in range(clusters)], axis=0)

        @pl.when(step < degree_top - 1)
        def _():
            @pl.when(step == 0)
            def _():
                for d in range(2):
                    drain(rq_recv.at[d], rq_sems.at[1, d])

            with_rhs = part + jnp.where(p == 0, 1.0, 0.0) * scaled
            for s in range(clusters):
                held[s] = with_rhs[s * rows : (s + 1) * rows]

            def answer(i):
                d = lax.div(i, pairs)
                e = lax.rem(i, pairs)
                parts = []
                for u in range(CAP):
                    total = jnp.zeros((rows, leaf), F32)
                    for s in range(clusters):
                        weight = rq_recv[d, e, u * clusters + s : u * clusters + s + 1, :]
                        weight = jnp.concatenate([weight] * (leaf // LANES), axis=1)
                        total = total + weight * held[s]
                    parts.append(total)
                sel_send[step, d, e] = jnp.concatenate(parts, axis=0).astype(WIRE)
                there = jnp.where(d == 0, down, up)
                device = {"clus": there, "pair": lax.rem(p + pairs - e, pairs)}
                send(sel_send.at[step, d, e], sel_recv.at[step, 1 - d, e],
                     sel_sems.at[0, step, d], sel_sems.at[1, step, 1 - d], device)

            each(0, 2 * pairs, answer)

        drain(s_recv.at[step], s_sems.at[1, step])
        sums = lax.fori_loop(0, group - 1, lambda d, t: t + s_recv[step, d], s_send[step, c], unroll=group <= 8)

        def apply(sums, places, basis):
            masked = jnp.concatenate(
                [jnp.where((lane >= s * rank) & (lane < (s + 1) * rank), sums, 0.0) for s in places], axis=0)
            both = jnp.dot(jnp.concatenate(split(masked), axis=0), basis, preferred_element_type=F32)
            return both[: len(places) * rows] + both[len(places) * rows :]

        @pl.when(step == 0)
        def _():
            for d in range(2):
                drain(u_recv.at[d], u_sems.at[1, d])

        for d in range(2):
            around = sums[2 * d * rows : (2 * d + 1) * rows]
            far_side[d] = apply(around, wanted[d * CAP : (d + 1) * CAP], u_recv[d])
        total = part + scaled + apply(sums[rows : 2 * rows], range(clusters), row_v[...])
        drain(n_recv.at[step], n_sems.at[1, step])
        for e in range(pairs - 1):
            total = total + n_recv[step, e].astype(F32)
        for s in range(clusters):
            result = total[s * rows : (s + 1) * rows]
            out[:, s * leaf : (s + 1) * leaf] = result
            xs[s] = result.astype(BF16).astype(F32)
        return unused

    lax.fori_loop(0, degree_top, product, 0)

    for d in range(2):
        drain(x0_send, x0_sems.at[0, d])
        drain(row_v, u_sems.at[0, d])
        drain(rq_recv.at[d], rq_sems.at[0, d])
    for step in range(degree_top):
        drain(s_recv.at[step], s_sems.at[0, step])
        drain(n_recv.at[step], n_sems.at[0, step])
        if step < degree_top - 1:
            for d in range(2):
                drain(sel_send.at[step, d], sel_sems.at[0, step, d])


def shards(
    clus, pairs, rhs_field, coefficients, near_blocks, near_tgt, near_src, row_basis, col_basis, far_src, far_tgt
):
    rows = rhs_field.shape[0]
    clusters, rank, leaf = row_basis.shape
    near_count, far_count = near_blocks.shape[0], col_basis.shape[0]
    degree_top = coefficients.shape[0] - 1
    chunk = clusters * rank
    sizes = (clus, pairs, clusters, rows, leaf, rank, near_count, far_count, degree_top)
    hbm = pl.BlockSpec(memory_space=pltpu.HBM)
    fields = clusters * rows
    rounds = degree_top
    return pl.pallas_call(
        functools.partial(kernel, sizes),
        out_shape=jax.ShapeDtypeStruct(rhs_field.shape, F32),
        in_specs=[hbm] * 9,
        out_specs=pl.BlockSpec(memory_space=pltpu.VMEM),
        scratch_shapes=[
            pltpu.SMEM(coefficients.shape, F32),
            pltpu.SMEM(near_tgt.shape, jnp.int32),
            pltpu.SMEM(near_src.shape, jnp.int32),
            pltpu.SMEM(far_src.shape, jnp.int32),
            pltpu.SMEM(far_tgt.shape, jnp.int32),
            pltpu.VMEM(rhs_field.shape, F32),
            pltpu.VMEM(near_blocks.shape, BF16),
            pltpu.VMEM((chunk, leaf), BF16),
            pltpu.VMEM((far_count * rank, leaf), BF16),
            pltpu.VMEM((clusters + 2 * CAP, rows, leaf), F32),
            pltpu.VMEM((fields, leaf), BF16),
            pltpu.VMEM((2, fields, leaf), BF16),
            pltpu.VMEM((2, clusters, rows, leaf), F32),
            pltpu.VMEM((2, CAP * clusters, LANES), F32),
            pltpu.VMEM((2, pairs, CAP * clusters, LANES), F32),
            pltpu.VMEM((2, chunk, leaf), BF16),
            pltpu.VMEM((2, CAP * rows, leaf), F32),
            pltpu.VMEM((far_count * rank // LANES, rows, LANES), jnp.int32),
            pltpu.VMEM((clusters, rows, leaf), F32),
            pltpu.VMEM((far_count * rank, clus * chunk), BF16),
            pltpu.VMEM((rounds, clus, 3 * rows, chunk), F32),
            pltpu.VMEM((rounds, clus * pairs - 1, 3 * rows, chunk), F32),
            pltpu.VMEM((rounds, fields, leaf), WIRE),
            pltpu.VMEM((rounds, pairs - 1, fields, leaf), WIRE),
            pltpu.VMEM((rounds - 1, 2, pairs, CAP * rows, leaf), WIRE),
            pltpu.VMEM((rounds - 1, 2, pairs, CAP * rows, leaf), WIRE),
            pltpu.SMEM((near_count,), jnp.int32),
            pltpu.SemaphoreType.DMA((9,)),
            pltpu.SemaphoreType.DMA((2, 2)),
            pltpu.SemaphoreType.DMA((2, 2)),
            pltpu.SemaphoreType.DMA((2, 2)),
            pltpu.SemaphoreType.DMA((2, rounds)),
            pltpu.SemaphoreType.DMA((2, rounds)),
            pltpu.SemaphoreType.DMA((2, rounds - 1, 2)),
        ],
        compiler_params=pltpu.CompilerParams(
            collective_id=0, has_side_effects=True, vmem_limit_bytes=63 * 1024 * 1024
        ),
        name="horner",
    )(
        coefficients, near_tgt, near_src, far_src, far_tgt, rhs_field,
        near_blocks, row_basis.reshape(chunk, leaf), col_basis.reshape(far_count * rank, leaf),
    )


def solution(mesh):
    return jax.shard_map(
        functools.partial(shards, mesh.shape["clus"], mesh.shape["pair"]),
        mesh=mesh,
        in_specs=(
            P("rhs", ("groups", "clus")),
            P(),
            P(("groups", "clus", "pair"), None, None),
            P(("groups", "clus", "pair")),
            P(("groups", "clus", "pair")),
            P(("groups", "clus"), None, None),
            P(("groups", "clus", "pair"), None, None),
            P(("groups", "clus", "pair")),
            P(("groups", "clus", "pair")),
        ),
        out_specs=P("rhs", ("groups", "clus")),
        check_vma=False,
    )
```

```python
import functools

import jax
import jax.numpy as jnp
from jax import lax
from jax.experimental import pallas as pl
from jax.experimental.pallas import tpu as pltpu
from jax.sharding import PartitionSpec as P

MESH = pl.DeviceIdType.MESH
F32 = jnp.float32
BF16 = jnp.bfloat16
CAP = 2
LANES = 128
NEAR_UNROLL = 16
WIRE = BF16


def drain(buffer, sem):
    pltpu.make_async_copy(buffer, buffer, sem).wait()


def split(value):
    high = value.astype(BF16)
    return high, (value - high.astype(F32)).astype(BF16)


def kernel(
    sizes, coeff_h, near_tgt_h, near_src_h, far_src_h, far_tgt_h, rhs_h, near_h, row_h, col_h, out,
    coeff, near_tgt, near_src, far_src, far_tgt, rhs, near_v, row_v, col_v,
    xs, x0_send, x0_recv, x0_wide, rq_send, rq_recv,
    u_recv, far_side, src_lane, held, fold, s_send, s_recv, n_send, n_recv, sel_send, sel_recv, index_s,
    load_sem, x0_sems, u_sems, rq_sems, s_sems, n_sems, sel_sems,
):
    clus, pairs, clusters, rows, leaf, rank, near_count, far_count, degree_top = sizes
    group = clus * pairs
    chunk = clusters * rank
    c = lax.axis_index("clus")
    p = lax.axis_index("pair")
    me = c * pairs + p
    up = lax.rem(c + 1, clus)
    down = lax.rem(c + clus - 1, clus)
    base = c * clusters
    beside = (down, up)

    places = (
        (coeff_h, coeff), (rhs_h, rhs), (far_tgt_h, far_tgt), (far_src_h, far_src), (near_src_h, near_src),
        (near_tgt_h, near_tgt), (col_h, col_v), (row_h, row_v), (near_h, near_v),
    )
    loads = [pltpu.make_async_copy(src, dst, load_sem.at[i]) for i, (src, dst) in enumerate(places)]
    for load in loads:
        load.start()

    def each(first, count, body):
        if count - first <= 2:
            for i in range(first, count):
                body(i)
        else:
            lax.fori_loop(first, count, lambda i, x: (body(i), x)[1], 0)

    def peer(d):
        other = lax.rem(me + d, group)
        return {"clus": lax.div(other, pairs), "pair": lax.rem(other, pairs)}

    barrier = pltpu.get_barrier_semaphore()
    each(1, group, lambda d: pl.semaphore_signal(barrier, inc=1, device_id=peer(d), device_id_type=MESH))

    def send(src, dst, send_sem, recv_sem, device):
        pltpu.make_async_remote_copy(
            src_ref=src, dst_ref=dst, send_sem=send_sem, recv_sem=recv_sem,
            device_id=device, device_id_type=MESH,
        ).start()

    for load in loads[:6]:
        load.wait()

    scale = coeff[degree_top]
    first = [(scale * rhs[:, s * leaf : (s + 1) * leaf]).astype(BF16).astype(F32) for s in range(clusters)]
    for s in range(clusters):
        xs[s] = first[s]
    x0_send[...] = jnp.concatenate(first, axis=0).astype(BF16)

    pl.semaphore_wait(barrier, group - 1)
    for d in range(2):
        send(x0_send, x0_recv.at[1 - d], x0_sems.at[0, d], x0_sems.at[1, 1 - d], {"clus": beside[d], "pair": p})
    def find(j, state):
        counts, wanted = list(state[:2]), list(state[2:])
        owner = lax.div(near_src[j], clusters)
        local = near_src[j] - owner * clusters
        place = local
        for d in range(2):
            here = owner == beside[d]
            for u in range(CAP):
                wanted[d * CAP + u] = jnp.where(here & (counts[d] == u), local, wanted[d * CAP + u])
            place = jnp.where(here, clusters + d * CAP + jnp.minimum(counts[d], CAP - 1), place)
            counts[d] = counts[d] + jnp.where(here, 1, 0)
        index_s[j] = place
        return (*counts, *wanted)

    wanted = lax.fori_loop(0, near_count, find, (jnp.int32(0),) * (2 + 2 * CAP))[2:]
    cluster_row = lax.broadcasted_iota(jnp.int32, (clusters, LANES), 0)
    for d in range(2):
        for u in range(CAP):
            rq_send[d, u * clusters : (u + 1) * clusters, :] = jnp.where(cluster_row == wanted[d * CAP + u], 1.0, 0.0)
    for d in range(2):
        def ask(e, d=d):
            device = {"clus": beside[d], "pair": lax.rem(p + e, pairs)}
            send(rq_send.at[d], rq_recv.at[1 - d, e], rq_sems.at[0, d], rq_sems.at[1, 1 - d], device)
        each(0, pairs, ask)
    loads[7].wait()
    for d in range(2):
        send(row_v, u_recv.at[1 - d], u_sems.at[0, d], u_sems.at[1, 1 - d], {"clus": beside[d], "pair": p})

    lane = lax.broadcasted_iota(jnp.int32, (rows, LANES), 1)
    per_tile = LANES // rank

    def mark_tile(q, unused):
        value = jnp.zeros((rows, LANES), jnp.int32)
        for i in range(per_tile):
            value = jnp.where(lane >= i * rank, far_src[q * per_tile + i] - base, value)
        src_lane[q] = value
        return unused

    lax.fori_loop(0, far_count // per_tile, mark_tile, 0)
    width = clus * chunk
    offset = lax.broadcasted_iota(jnp.int32, (rank, width), 1) - lax.broadcasted_iota(jnp.int32, (rank, width), 0)

    def place_block(j, unused):
        start = pl.multiple_of(j * rank, rank)
        fold[pl.ds(start, rank), :] = jnp.where(offset == far_tgt[j] * rank, 1.0, 0.0).astype(BF16)
        return unused

    lax.fori_loop(0, far_count, place_block, 0, unroll=2)
    loads[6].wait()

    contract_last = (((1,), (1,)), ((), ()))
    tile_lanes = far_count // per_tile

    def product(step, unused):
        degree = degree_top - 1 - step

        own = jnp.concatenate([xs[s] for s in range(clusters)], axis=0).astype(BF16)
        every = lax.dot_general(own, col_v[...], contract_last, preferred_element_type=F32)
        parts = []
        for q in range(tile_lanes):
            source_of = src_lane[q]
            total = jnp.zeros((rows, LANES), F32)
            for s in range(clusters):
                piece = every[s * rows : (s + 1) * rows, q * LANES : (q + 1) * LANES]
                total = total + jnp.where(source_of == s, piece, 0.0)
            parts.append(total)
        coef = jnp.concatenate(parts, axis=1)
        both = jnp.dot(jnp.concatenate(split(coef), axis=0), fold[...], preferred_element_type=F32)
        mine = both[:rows] + both[rows:]
        chunks = [mine[:, i * chunk : (i + 1) * chunk] for i in range(clus)]
        for i in range(clus):
            s_send[step, i] = jnp.concatenate([chunks[(i + k) % clus] for k in (-1, 0, 1)], axis=0)

        def spread(d):
            device = peer(d)
            send(s_send.at[step, device["clus"]], s_recv.at[step, d - 1], s_sems.at[0, step], s_sems.at[1, step], device)

        each(1, group, spread)

        @pl.when(step == 0)
        def _():
            for d in range(2):
                drain(x0_recv.at[d], x0_sems.at[1, d])
                wide = x0_recv[d].astype(F32)
                for s in range(clusters):
                    x0_wide[d, s] = wide[s * rows : (s + 1) * rows]
                for u in range(CAP):
                    xs[clusters + d * CAP + u] = x0_wide[d, wanted[d * CAP + u]]
            loads[8].wait()

        @pl.when(step > 0)
        def _():
            for d in range(2):
                drain(sel_recv.at[step - 1, d], sel_sems.at[1, step - 1, d])
                value = far_side[d]
                for e in range(pairs):
                    value = value + sel_recv[step - 1, d, e].astype(F32)
                for u in range(CAP):
                    xs[clusters + d * CAP + u] = value[u * rows : (u + 1) * rows].astype(BF16).astype(F32)

        def near_block(i, near):
            near = list(near)
            for k in range(NEAR_UNROLL):
                j = i * NEAR_UNROLL + k
                value = lax.dot_general(
                    xs[index_s[j]].astype(BF16), near_v[j], contract_last, preferred_element_type=F32)
                target = near_tgt[j] - base
                for s in range(clusters):
                    near[s] = near[s] + value * jnp.where(target == s, 1.0, 0.0)
            return tuple(near)

        near = lax.fori_loop(
            0, near_count // NEAR_UNROLL, near_block,
            tuple(jnp.zeros((rows, leaf), F32) for s in range(clusters)))

        part = jnp.concatenate(near, axis=0)
        n_send[step] = part.astype(WIRE)

        def share(e):
            send(n_send.at[step], n_recv.at[step, e - 1], n_sems.at[0, step], n_sems.at[1, step],
                 {"clus": c, "pair": lax.rem(p + e, pairs)})

        each(1, pairs, share)
        scaled = jnp.concatenate([coeff[degree] * rhs[:, s * leaf : (s + 1) * leaf] for s in range(clusters)], axis=0)

        @pl.when(step < degree_top - 1)
        def _():
            @pl.when(step == 0)
            def _():
                for d in range(2):
                    drain(rq_recv.at[d], rq_sems.at[1, d])

            with_rhs = part + jnp.where(p == 0, 1.0, 0.0) * scaled
            for s in range(clusters):
                held[s] = with_rhs[s * rows : (s + 1) * rows]

            def answer(i):
                d = lax.div(i, pairs)
                e = lax.rem(i, pairs)
                parts = []
                for u in range(CAP):
                    total = jnp.zeros((rows, leaf), F32)
                    for s in range(clusters):
                        weight = rq_recv[d, e, u * clusters + s : u * clusters + s + 1, :]
                        weight = jnp.concatenate([weight] * (leaf // LANES), axis=1)
                        total = total + weight * held[s]
                    parts.append(total)
                sel_send[step, d, e] = jnp.concatenate(parts, axis=0).astype(WIRE)
                there = jnp.where(d == 0, down, up)
                device = {"clus": there, "pair": lax.rem(p + pairs - e, pairs)}
                send(sel_send.at[step, d, e], sel_recv.at[step, 1 - d, e],
                     sel_sems.at[0, step, d], sel_sems.at[1, step, 1 - d], device)

            each(0, 2 * pairs, answer)

        drain(s_recv.at[step], s_sems.at[1, step])
        sums = lax.fori_loop(0, group - 1, lambda d, t: t + s_recv[step, d], s_send[step, c], unroll=group <= 8)

        def apply(sums, places, basis):
            masked = jnp.concatenate(
                [jnp.where((lane >= s * rank) & (lane < (s + 1) * rank), sums, 0.0) for s in places], axis=0)
            both = jnp.dot(jnp.concatenate(split(masked), axis=0), basis, preferred_element_type=F32)
            return both[: len(places) * rows] + both[len(places) * rows :]

        @pl.when(step == 0)
        def _():
            for d in range(2):
                drain(u_recv.at[d], u_sems.at[1, d])

        for d in range(2):
            around = sums[2 * d * rows : (2 * d + 1) * rows]
            far_side[d] = apply(around, wanted[d * CAP : (d + 1) * CAP], u_recv[d])
        total = part + scaled + apply(sums[rows : 2 * rows], range(clusters), row_v[...])
        drain(n_recv.at[step], n_sems.at[1, step])
        for e in range(pairs - 1):
            total = total + n_recv[step, e].astype(F32)
        for s in range(clusters):
            result = total[s * rows : (s + 1) * rows]
            out[:, s * leaf : (s + 1) * leaf] = result
            xs[s] = result.astype(BF16).astype(F32)
        return unused

    lax.fori_loop(0, degree_top, product, 0)

    for d in range(2):
        drain(x0_send, x0_sems.at[0, d])
        drain(row_v, u_sems.at[0, d])
        drain(rq_recv.at[d], rq_sems.at[0, d])
    for step in range(degree_top):
        drain(s_recv.at[step], s_sems.at[0, step])
        drain(n_recv.at[step], n_sems.at[0, step])
        if step < degree_top - 1:
            for d in range(2):
                drain(sel_send.at[step, d], sel_sems.at[0, step, d])


def shards(
    clus, pairs, rhs_field, coefficients, near_blocks, near_tgt, near_src, row_basis, col_basis, far_src, far_tgt
):
    rows = rhs_field.shape[0]
    clusters, rank, leaf = row_basis.shape
    near_count, far_count = near_blocks.shape[0], col_basis.shape[0]
    degree_top = coefficients.shape[0] - 1
    chunk = clusters * rank
    sizes = (clus, pairs, clusters, rows, leaf, rank, near_count, far_count, degree_top)
    hbm = pl.BlockSpec(memory_space=pltpu.HBM)
    fields = clusters * rows
    rounds = degree_top
    return pl.pallas_call(
        functools.partial(kernel, sizes),
        out_shape=jax.ShapeDtypeStruct(rhs_field.shape, F32),
        in_specs=[hbm] * 9,
        out_specs=pl.BlockSpec(memory_space=pltpu.VMEM),
        scratch_shapes=[
            pltpu.SMEM(coefficients.shape, F32),
            pltpu.SMEM(near_tgt.shape, jnp.int32),
            pltpu.SMEM(near_src.shape, jnp.int32),
            pltpu.SMEM(far_src.shape, jnp.int32),
            pltpu.SMEM(far_tgt.shape, jnp.int32),
            pltpu.VMEM(rhs_field.shape, F32),
            pltpu.VMEM(near_blocks.shape, BF16),
            pltpu.VMEM((chunk, leaf), BF16),
            pltpu.VMEM((far_count * rank, leaf), BF16),
            pltpu.VMEM((clusters + 2 * CAP, rows, leaf), F32),
            pltpu.VMEM((fields, leaf), BF16),
            pltpu.VMEM((2, fields, leaf), BF16),
            pltpu.VMEM((2, clusters, rows, leaf), F32),
            pltpu.VMEM((2, CAP * clusters, LANES), F32),
            pltpu.VMEM((2, pairs, CAP * clusters, LANES), F32),
            pltpu.VMEM((2, chunk, leaf), BF16),
            pltpu.VMEM((2, CAP * rows, leaf), F32),
            pltpu.VMEM((far_count * rank // LANES, rows, LANES), jnp.int32),
            pltpu.VMEM((clusters, rows, leaf), F32),
            pltpu.VMEM((far_count * rank, clus * chunk), BF16),
            pltpu.VMEM((rounds, clus, 3 * rows, chunk), F32),
            pltpu.VMEM((rounds, clus * pairs - 1, 3 * rows, chunk), F32),
            pltpu.VMEM((rounds, fields, leaf), WIRE),
            pltpu.VMEM((rounds, pairs - 1, fields, leaf), WIRE),
            pltpu.VMEM((rounds - 1, 2, pairs, CAP * rows, leaf), WIRE),
            pltpu.VMEM((rounds - 1, 2, pairs, CAP * rows, leaf), WIRE),
            pltpu.SMEM((near_count,), jnp.int32),
            pltpu.SemaphoreType.DMA((9,)),
            pltpu.SemaphoreType.DMA((2, 2)),
            pltpu.SemaphoreType.DMA((2, 2)),
            pltpu.SemaphoreType.DMA((2, 2)),
            pltpu.SemaphoreType.DMA((2, rounds)),
            pltpu.SemaphoreType.DMA((2, rounds)),
            pltpu.SemaphoreType.DMA((2, rounds - 1, 2)),
        ],
        compiler_params=pltpu.CompilerParams(
            collective_id=0, has_side_effects=True, vmem_limit_bytes=63 * 1024 * 1024
        ),
        name="horner",
    )(
        coefficients, near_tgt, near_src, far_src, far_tgt, rhs_field,
        near_blocks, row_basis.reshape(chunk, leaf), col_basis.reshape(far_count * rank, leaf),
    )


def solution(mesh):
    return jax.shard_map(
        functools.partial(shards, mesh.shape["clus"], mesh.shape["pair"]),
        mesh=mesh,
        in_specs=(
            P("rhs", ("groups", "clus")),
            P(),
            P(("groups", "clus", "pair"), None, None),
            P(("groups", "clus", "pair")),
            P(("groups", "clus", "pair")),
            P(("groups", "clus"), None, None),
            P(("groups", "clus", "pair"), None, None),
            P(("groups", "clus", "pair")),
            P(("groups", "clus", "pair")),
        ),
        out_specs=P("rhs", ("groups", "clus")),
        check_vma=False,
    )
```

```python
import functools

import jax
import jax.numpy as jnp
from jax import lax
from jax.experimental import pallas as pl
from jax.experimental.pallas import tpu as pltpu
from jax.sharding import PartitionSpec as P

MESH = pl.DeviceIdType.MESH
F32 = jnp.float32
BF16 = jnp.bfloat16
CAP = 2
LANES = 128
NEAR_UNROLL = 16
WIRE = BF16


def drain(buffer, sem):
    pltpu.make_async_copy(buffer, buffer, sem).wait()


def split(value):
    high = value.astype(BF16)
    return high, (value - high.astype(F32)).astype(BF16)


def kernel(
    sizes, coeff_h, near_tgt_h, near_src_h, far_src_h, far_tgt_h, rhs_h, near_h, row_h, col_h, out,
    coeff, near_tgt, near_src, far_src, far_tgt, rhs, near_v, row_v, col_v,
    xs, x0_send, x0_recv, x0_wide, rq_send, rq_recv,
    u_recv, far_side, src_lane, held, fold, s_send, s_recv, n_send, n_recv, sel_send, sel_recv, index_s,
    load_sem, x0_sems, u_sems, rq_sems, s_sems, n_sems, sel_sems,
):
    clus, pairs, clusters, rows, leaf, rank, near_count, far_count, degree_top = sizes
    group = clus * pairs
    chunk = clusters * rank
    c = lax.axis_index("clus")
    p = lax.axis_index("pair")
    me = c * pairs + p
    up = lax.rem(c + 1, clus)
    down = lax.rem(c + clus - 1, clus)
    base = c * clusters
    beside = (down, up)

    places = (
        (coeff_h, coeff), (rhs_h, rhs), (far_tgt_h, far_tgt), (far_src_h, far_src), (near_src_h, near_src),
        (near_tgt_h, near_tgt), (col_h, col_v), (row_h, row_v), (near_h, near_v),
    )
    loads = [pltpu.make_async_copy(src, dst, load_sem.at[i]) for i, (src, dst) in enumerate(places)]
    for load in loads:
        load.start()

    def each(first, count, body):
        if count - first <= 2:
            for i in range(first, count):
                body(i)
        else:
            lax.fori_loop(first, count, lambda i, x: (body(i), x)[1], 0)

    def peer(d):
        other = lax.rem(me + d, group)
        return {"clus": lax.div(other, pairs), "pair": lax.rem(other, pairs)}

    barrier = pltpu.get_barrier_semaphore()
    each(1, group, lambda d: pl.semaphore_signal(barrier, inc=1, device_id=peer(d), device_id_type=MESH))

    def send(src, dst, send_sem, recv_sem, device):
        pltpu.make_async_remote_copy(
            src_ref=src, dst_ref=dst, send_sem=send_sem, recv_sem=recv_sem,
            device_id=device, device_id_type=MESH,
        ).start()

    for load in loads[:6]:
        load.wait()

    scale = coeff[degree_top]
    first = [(scale * rhs[:, s * leaf : (s + 1) * leaf]).astype(BF16).astype(F32) for s in range(clusters)]
    for s in range(clusters):
        xs[s] = first[s]
    x0_send[...] = jnp.concatenate(first, axis=0).astype(BF16)

    pl.semaphore_wait(barrier, group - 1)
    for d in range(2):
        send(x0_send, x0_recv.at[1 - d], x0_sems.at[0, d], x0_sems.at[1, 1 - d], {"clus": beside[d], "pair": p})
    def find(j, state):
        counts, wanted = list(state[:2]), list(state[2:])
        owner = lax.div(near_src[j], clusters)
        local = near_src[j] - owner * clusters
        place = local
        for d in range(2):
            here = owner == beside[d]
            for u in range(CAP):
                wanted[d * CAP + u] = jnp.where(here & (counts[d] == u), local, wanted[d * CAP + u])
            place = jnp.where(here, clusters + d * CAP + jnp.minimum(counts[d], CAP - 1), place)
            counts[d] = counts[d] + jnp.where(here, 1, 0)
        index_s[j] = place
        return (*counts, *wanted)

    wanted = lax.fori_loop(0, near_count, find, (jnp.int32(0),) * (2 + 2 * CAP))[2:]
    cluster_row = lax.broadcasted_iota(jnp.int32, (clusters, LANES), 0)
    for d in range(2):
        for u in range(CAP):
            rq_send[d, u * clusters : (u + 1) * clusters, :] = jnp.where(cluster_row == wanted[d * CAP + u], 1.0, 0.0)
    for d in range(2):
        def ask(e, d=d):
            device = {"clus": beside[d], "pair": lax.rem(p + e, pairs)}
            send(rq_send.at[d], rq_recv.at[1 - d, e], rq_sems.at[0, d], rq_sems.at[1, 1 - d], device)
        each(0, pairs, ask)
    loads[7].wait()
    for d in range(2):
        send(row_v, u_recv.at[1 - d], u_sems.at[0, d], u_sems.at[1, 1 - d], {"clus": beside[d], "pair": p})

    lane = lax.broadcasted_iota(jnp.int32, (rows, LANES), 1)
    per_tile = LANES // rank

    def mark_tile(q, unused):
        value = jnp.zeros((rows, LANES), jnp.int32)
        for i in range(per_tile):
            value = jnp.where(lane >= i * rank, far_src[q * per_tile + i] - base, value)
        src_lane[q] = value
        return unused

    lax.fori_loop(0, far_count // per_tile, mark_tile, 0)
    width = clus * chunk
    offset = lax.broadcasted_iota(jnp.int32, (rank, width), 1) - lax.broadcasted_iota(jnp.int32, (rank, width), 0)

    def place_block(j, unused):
        start = pl.multiple_of(j * rank, rank)
        fold[pl.ds(start, rank), :] = jnp.where(offset == far_tgt[j] * rank, 1.0, 0.0).astype(BF16)
        return unused

    lax.fori_loop(0, far_count, place_block, 0, unroll=8)
    loads[6].wait()

    contract_last = (((1,), (1,)), ((), ()))
    tile_lanes = far_count // per_tile

    def product(step, unused):
        degree = degree_top - 1 - step

        own = jnp.concatenate([xs[s] for s in range(clusters)], axis=0).astype(BF16)
        every = lax.dot_general(own, col_v[...], contract_last, preferred_element_type=F32)
        parts = []
        for q in range(tile_lanes):
            source_of = src_lane[q]
            total = jnp.zeros((rows, LANES), F32)
            for s in range(clusters):
                piece = every[s * rows : (s + 1) * rows, q * LANES : (q + 1) * LANES]
                total = total + jnp.where(source_of == s, piece, 0.0)
            parts.append(total)
        coef = jnp.concatenate(parts, axis=1)
        both = jnp.dot(jnp.concatenate(split(coef), axis=0), fold[...], preferred_element_type=F32)
        mine = both[:rows] + both[rows:]
        chunks = [mine[:, i * chunk : (i + 1) * chunk] for i in range(clus)]
        for i in range(clus):
            s_send[step, i] = jnp.concatenate([chunks[(i + k) % clus] for k in (-1, 0, 1)], axis=0)

        def spread(d):
            device = peer(d)
            send(s_send.at[step, device["clus"]], s_recv.at[step, d - 1], s_sems.at[0, step], s_sems.at[1, step], device)

        each(1, group, spread)

        @pl.when(step == 0)
        def _():
            for d in range(2):
                drain(x0_recv.at[d], x0_sems.at[1, d])
                wide = x0_recv[d].astype(F32)
                for s in range(clusters):
                    x0_wide[d, s] = wide[s * rows : (s + 1) * rows]
                for u in range(CAP):
                    xs[clusters + d * CAP + u] = x0_wide[d, wanted[d * CAP + u]]
            loads[8].wait()

        @pl.when(step > 0)
        def _():
            for d in range(2):
                drain(sel_recv.at[step - 1, d], sel_sems.at[1, step - 1, d])
                value = far_side[d]
                for e in range(pairs):
                    value = value + sel_recv[step - 1, d, e].astype(F32)
                for u in range(CAP):
                    xs[clusters + d * CAP + u] = value[u * rows : (u + 1) * rows].astype(BF16).astype(F32)

        def near_block(i, near):
            near = list(near)
            for k in range(NEAR_UNROLL):
                j = i * NEAR_UNROLL + k
                value = lax.dot_general(
                    xs[index_s[j]].astype(BF16), near_v[j], contract_last, preferred_element_type=F32)
                target = near_tgt[j] - base
                for s in range(clusters):
                    near[s] = near[s] + value * jnp.where(target == s, 1.0, 0.0)
            return tuple(near)

        near = lax.fori_loop(
            0, near_count // NEAR_UNROLL, near_block,
            tuple(jnp.zeros((rows, leaf), F32) for s in range(clusters)))

        part = jnp.concatenate(near, axis=0)
        n_send[step] = part.astype(WIRE)

        def share(e):
            send(n_send.at[step], n_recv.at[step, e - 1], n_sems.at[0, step], n_sems.at[1, step],
                 {"clus": c, "pair": lax.rem(p + e, pairs)})

        each(1, pairs, share)
        scaled = jnp.concatenate([coeff[degree] * rhs[:, s * leaf : (s + 1) * leaf] for s in range(clusters)], axis=0)

        @pl.when(step < degree_top - 1)
        def _():
            @pl.when(step == 0)
            def _():
                for d in range(2):
                    drain(rq_recv.at[d], rq_sems.at[1, d])

            with_rhs = part + jnp.where(p == 0, 1.0, 0.0) * scaled
            for s in range(clusters):
                held[s] = with_rhs[s * rows : (s + 1) * rows]

            def answer(i):
                d = lax.div(i, pairs)
                e = lax.rem(i, pairs)
                parts = []
                for u in range(CAP):
                    total = jnp.zeros((rows, leaf), F32)
                    for s in range(clusters):
                        weight = rq_recv[d, e, u * clusters + s : u * clusters + s + 1, :]
                        weight = jnp.concatenate([weight] * (leaf // LANES), axis=1)
                        total = total + weight * held[s]
                    parts.append(total)
                sel_send[step, d, e] = jnp.concatenate(parts, axis=0).astype(WIRE)
                there = jnp.where(d == 0, down, up)
                device = {"clus": there, "pair": lax.rem(p + pairs - e, pairs)}
                send(sel_send.at[step, d, e], sel_recv.at[step, 1 - d, e],
                     sel_sems.at[0, step, d], sel_sems.at[1, step, 1 - d], device)

            each(0, 2 * pairs, answer)

        drain(s_recv.at[step], s_sems.at[1, step])
        sums = lax.fori_loop(0, group - 1, lambda d, t: t + s_recv[step, d], s_send[step, c], unroll=group <= 8)

        def apply(sums, places, basis):
            masked = jnp.concatenate(
                [jnp.where((lane >= s * rank) & (lane < (s + 1) * rank), sums, 0.0) for s in places], axis=0)
            both = jnp.dot(jnp.concatenate(split(masked), axis=0), basis, preferred_element_type=F32)
            return both[: len(places) * rows] + both[len(places) * rows :]

        @pl.when(step == 0)
        def _():
            for d in range(2):
                drain(u_recv.at[d], u_sems.at[1, d])

        @pl.when(step < degree_top - 1)
        def _():
            for d in range(2):
                around = sums[2 * d * rows : (2 * d + 1) * rows]
                far_side[d] = apply(around, wanted[d * CAP : (d + 1) * CAP], u_recv[d])

        total = part + scaled + apply(sums[rows : 2 * rows], range(clusters), row_v[...])
        drain(n_recv.at[step], n_sems.at[1, step])
        for e in range(pairs - 1):
            total = total + n_recv[step, e].astype(F32)
        for s in range(clusters):
            result = total[s * rows : (s + 1) * rows]
            out[:, s * leaf : (s + 1) * leaf] = result
            xs[s] = result.astype(BF16).astype(F32)
        return unused

    lax.fori_loop(0, degree_top, product, 0)

    for d in range(2):
        drain(x0_send, x0_sems.at[0, d])
        drain(row_v, u_sems.at[0, d])
        drain(rq_recv.at[d], rq_sems.at[0, d])
    for step in range(degree_top):
        drain(s_recv.at[step], s_sems.at[0, step])
        drain(n_recv.at[step], n_sems.at[0, step])
        if step < degree_top - 1:
            for d in range(2):
                drain(sel_send.at[step, d], sel_sems.at[0, step, d])


def shards(
    clus, pairs, rhs_field, coefficients, near_blocks, near_tgt, near_src, row_basis, col_basis, far_src, far_tgt
):
    rows = rhs_field.shape[0]
    clusters, rank, leaf = row_basis.shape
    near_count, far_count = near_blocks.shape[0], col_basis.shape[0]
    degree_top = coefficients.shape[0] - 1
    chunk = clusters * rank
    sizes = (clus, pairs, clusters, rows, leaf, rank, near_count, far_count, degree_top)
    hbm = pl.BlockSpec(memory_space=pltpu.HBM)
    fields = clusters * rows
    rounds = degree_top
    return pl.pallas_call(
        functools.partial(kernel, sizes),
        out_shape=jax.ShapeDtypeStruct(rhs_field.shape, F32),
        in_specs=[hbm] * 9,
        out_specs=pl.BlockSpec(memory_space=pltpu.VMEM),
        scratch_shapes=[
            pltpu.SMEM(coefficients.shape, F32),
            pltpu.SMEM(near_tgt.shape, jnp.int32),
            pltpu.SMEM(near_src.shape, jnp.int32),
            pltpu.SMEM(far_src.shape, jnp.int32),
            pltpu.SMEM(far_tgt.shape, jnp.int32),
            pltpu.VMEM(rhs_field.shape, F32),
            pltpu.VMEM(near_blocks.shape, BF16),
            pltpu.VMEM((chunk, leaf), BF16),
            pltpu.VMEM((far_count * rank, leaf), BF16),
            pltpu.VMEM((clusters + 2 * CAP, rows, leaf), F32),
            pltpu.VMEM((fields, leaf), BF16),
            pltpu.VMEM((2, fields, leaf), BF16),
            pltpu.VMEM((2, clusters, rows, leaf), F32),
            pltpu.VMEM((2, CAP * clusters, LANES), F32),
            pltpu.VMEM((2, pairs, CAP * clusters, LANES), F32),
            pltpu.VMEM((2, chunk, leaf), BF16),
            pltpu.VMEM((2, CAP * rows, leaf), F32),
            pltpu.VMEM((far_count * rank // LANES, rows, LANES), jnp.int32),
            pltpu.VMEM((clusters, rows, leaf), F32),
            pltpu.VMEM((far_count * rank, clus * chunk), BF16),
            pltpu.VMEM((rounds, clus, 3 * rows, chunk), F32),
            pltpu.VMEM((rounds, clus * pairs - 1, 3 * rows, chunk), F32),
            pltpu.VMEM((rounds, fields, leaf), WIRE),
            pltpu.VMEM((rounds, pairs - 1, fields, leaf), WIRE),
            pltpu.VMEM((rounds - 1, 2, pairs, CAP * rows, leaf), WIRE),
            pltpu.VMEM((rounds - 1, 2, pairs, CAP * rows, leaf), WIRE),
            pltpu.SMEM((near_count,), jnp.int32),
            pltpu.SemaphoreType.DMA((9,)),
            pltpu.SemaphoreType.DMA((2, 2)),
            pltpu.SemaphoreType.DMA((2, 2)),
            pltpu.SemaphoreType.DMA((2, 2)),
            pltpu.SemaphoreType.DMA((2, rounds)),
            pltpu.SemaphoreType.DMA((2, rounds)),
            pltpu.SemaphoreType.DMA((2, rounds - 1, 2)),
        ],
        compiler_params=pltpu.CompilerParams(
            collective_id=0, has_side_effects=True, vmem_limit_bytes=63 * 1024 * 1024
        ),
        name="horner",
    )(
        coefficients, near_tgt, near_src, far_src, far_tgt, rhs_field,
        near_blocks, row_basis.reshape(chunk, leaf), col_basis.reshape(far_count * rank, leaf),
    )


def solution(mesh):
    return jax.shard_map(
        functools.partial(shards, mesh.shape["clus"], mesh.shape["pair"]),
        mesh=mesh,
        in_specs=(
            P("rhs", ("groups", "clus")),
            P(),
            P(("groups", "clus", "pair"), None, None),
            P(("groups", "clus", "pair")),
            P(("groups", "clus", "pair")),
            P(("groups", "clus"), None, None),
            P(("groups", "clus", "pair"), None, None),
            P(("groups", "clus", "pair")),
            P(("groups", "clus", "pair")),
        ),
        out_specs=P("rhs", ("groups", "clus")),
        check_vma=False,
    )
```
